32 devices in a mesh: sec: 2 (over core), clu: 4 (over y, x), blk: 4 (over z).
Axes of the slice: x: 2, y: 2, z: 4, core: 2. Of those that a mesh axis runs over, the one named last changes fastest.
Arguments:
- right_side: float32 [32, 64, 32, 128], P(None, ('sec', 'clu'), 'blk'), may hold values from -18 to 18
- block_weight: float32 [64, 32], P(('sec', 'clu'), 'blk'), may hold values from 2 to 8
- across_weight: float32 [64, 32], P(('sec', 'clu'), 'blk'), may hold values from 0.3 to 1
- along_weight: float32 [64, 32], P(('sec', 'clu'), 'blk'), may hold values from 0.3 to 1
- block_stiffness: bfloat16 [128, 128], replicated, may hold values from -0.1 to 1.1, as said below
- across_matrix: bfloat16 [128, 128], replicated, may hold values from -0.044194174 to 0.044194174
- along_matrix: bfloat16 [128, 128], replicated, may hold values from -0.044194174 to 0.044194174
- boundary_blocks: bfloat16 [2, 4, 192, 128, 128], P('sec', 'clu', 'blk'), may hold values from -0.22949219 to 0.22949219
- block_rows: int32 [2, 4, 192], P('sec', 'clu', 'blk'), may hold values from 0 to 7
- block_columns: int32 [2, 4, 192], P('sec', 'clu', 'blk'), may hold values from 0 to 7
- live_pairs: int32 [2, 4, 4], P('sec', 'clu', 'blk'), may hold values from 12 to 48, as said below
- surface_index: int32 [2, 4, 512], P('sec', 'clu', 'blk'), may hold values from 0 to 8191, as said below
- interface_slot: int32 [4096], P('clu'), may hold values from 0 to 1023, as said below
Outputs:
- solution: float32 [32, 64, 32, 128], P(None, ('sec', 'clu'), 'blk')
The draws below stay inside these ranges and needn't reach their ends.
Inputs may be any that keep to these rules, and one draw needn't show every extreme that they name: `block_stiffness`: symmetric. The first live_pairs[s, c, j] of a device's 48 listed pairs are live; some device has all 48 live. `surface_index`: the 128 entries of one device are distinct local dof numbers of that device. `interface_slot`: within each row range of 1024 interface dofs, each slot is taken exactly once.
All inputs are finite; a program needn't handle non-finite values.
Results may differ from the reference program's by a relative error of at most 0.0003.
The reference program's roundings to bfloat16 on the way count: a program that leaves them out, or rounds other values in their place, can miss the bound.
Values may be sent and summed in bfloat16 or wider, within the bound.
A program may use at most 64 MiB of HBM per device.

```python
import math
import jax
import jax.numpy as jnp
from jax import lax

P_SIZE = 128
CL = 128
CASES = 32
BX = 8
BY = 8
SURF = 128
NP = 48
ITERS = 3
NBX = 64
NBY = 32
RROWS = 1024
RCL = 8
CCL = 8
N_SEC = 2
N_CLU = 4
N_BLK = 4


def draw_block_stiffness(key, part):
    noise = jax.random.truncated_normal(key, -4.0, 4.0, (P_SIZE, P_SIZE), jnp.float32) * (0.2 / math.sqrt(2.0 * P_SIZE))
    return (jnp.eye(P_SIZE, dtype=jnp.float32) + noise + noise.T).astype(jnp.bfloat16)


def draw_across_matrix(key, part):
    return (jax.random.truncated_normal(jax.random.fold_in(key, 11), -4.0, 4.0, (P_SIZE, P_SIZE), jnp.float32) * (0.125 / math.sqrt(P_SIZE))).astype(jnp.bfloat16)


def draw_along_matrix(key, part):
    return (jax.random.truncated_normal(jax.random.fold_in(key, 23), -4.0, 4.0, (P_SIZE, P_SIZE), jnp.float32) * (0.125 / math.sqrt(P_SIZE))).astype(jnp.bfloat16)


def draw_live_pairs(key, part):
    device_count = N_SEC * N_CLU * N_BLK
    lowest = max(1, NP // 4)
    counts = jax.random.randint(jax.random.fold_in(key, 1), (device_count,), lowest, NP + 1)
    busiest = jax.random.randint(jax.random.fold_in(key, 2), (), 0, device_count)
    counts = counts.at[busiest].set(NP)
    counts = counts.at[(busiest + 1) % device_count].set(lowest)
    return counts.reshape(N_SEC, N_CLU, N_BLK).astype(jnp.int32)


def draw_surface_index(key, part):
    dof_total = BX * BY * P_SIZE
    device_count = N_SEC * N_CLU * N_BLK
    split_keys = jax.random.split(jax.random.fold_in(key, 3), device_count)
    chosen = jax.vmap(lambda subkey: jax.random.permutation(subkey, dof_total)[:SURF])(split_keys).astype(jnp.int32)
    leading = chosen[0]
    present = jnp.any(leading == dof_total - 1)
    leading = jnp.where(present, leading, leading.at[0].set(dof_total - 1))
    chosen = chosen.at[0].set(leading)
    return chosen.reshape(N_SEC, N_CLU, N_BLK * SURF)


def draw_interface_slot(key, part):
    split_keys = jax.random.split(jax.random.fold_in(key, 5), N_CLU)
    orders = jax.vmap(lambda subkey: jax.random.permutation(subkey, RROWS))(split_keys)
    return orders.reshape(N_CLU * RROWS).astype(jnp.int32)


def touch_ends(array, key, low, top_value):
    dims = array.shape
    place = [jax.random.randint(jax.random.fold_in(key, axis), (), 0, dims[axis]) for axis in range(len(dims))]
    array = array.at[tuple(place)].set(low)
    longest = dims.index(max(dims))
    place[longest] = (place[longest] + 1) % dims[longest]
    return array.at[tuple(place)].set(top_value)


def steps_of(own_key, dims, cuts, low, top_value):
    gain = 1.0
    for position, parts in cuts:
        draws = jax.random.uniform(jax.random.fold_in(jax.random.fold_in(own_key, 6), position), (parts,), jnp.float32, low / len(cuts), top_value / len(cuts))
        gain = gain * jnp.repeat(jnp.exp(draws), dims[position] // parts).reshape((-1,) + (1,) * (len(dims) - 1 - position))
    return gain


def bell_draw(stream_key, shape, deviation, bound, shards=(), kind=jnp.bfloat16):
    values = deviation * jax.random.normal(stream_key, shape, jnp.float32)
    if shards:
        values = values * steps_of(stream_key, shape, shards, -0.22, 0.18)
    return jnp.clip(values, -bound, bound).astype(kind)


def setup_inputs(seed: int = 0) -> dict:
    keys = jax.random.split(jax.random.key(seed), 14)
    right_side = bell_draw(keys[0], (CASES, NBX, NBY, P_SIZE), 3.0, 18.0, ((1, 8), (2, 4)), jnp.float32)
    block_weight = jnp.clip(jnp.exp(math.log(8.0) - 1.3862944 * jax.random.uniform(keys[1], (NBX, NBY), jnp.float32) ** steps_of(keys[1], (NBX, NBY), ((0, 8), (1, 4)), -0.2, 0.2)), 2.0, 8.0)
    across_weight = jnp.clip(jnp.exp(math.log(1.0) - 1.2039728 * jax.random.uniform(keys[2], (NBX, NBY), jnp.float32) ** steps_of(keys[2], (NBX, NBY), ((0, 8), (1, 4)), -0.2, 0.2)), 0.3, 1.0)
    along_weight = jnp.clip(jnp.exp(math.log(1.0) - 1.2039728 * jax.random.uniform(keys[3], (NBX, NBY), jnp.float32) ** steps_of(keys[3], (NBX, NBY), ((0, 8), (1, 4)), -0.2, 0.2)), 0.3, 1.0)
    block_stiffness = draw_block_stiffness(jax.random.fold_in(keys[13], 71), 0)
    across_matrix = draw_across_matrix(jax.random.fold_in(keys[13], 71), 0)
    along_matrix = draw_along_matrix(jax.random.fold_in(keys[13], 71), 0)
    boundary_blocks = bell_draw(keys[7], (N_SEC, N_CLU, N_BLK * NP, CL, CL), (3 * (CL * CL * NP / SURF) ** -0.5), 0.22949219, ((0, 2), (1, 4), (2, 4)))
    block_rows = touch_ends(jax.random.randint(keys[8], (N_SEC, N_CLU, N_BLK * NP), 0, RCL), jax.random.fold_in(keys[8], 1), 0, RCL - 1).astype(jnp.int32)
    block_columns = touch_ends(jax.random.randint(keys[9], (N_SEC, N_CLU, N_BLK * NP), 0, CCL), jax.random.fold_in(keys[9], 1), 0, CCL - 1).astype(jnp.int32)
    live_pairs = draw_live_pairs(jax.random.fold_in(keys[13], 71), 0)
    surface_index = draw_surface_index(jax.random.fold_in(keys[13], 71), 0)
    interface_slot = draw_interface_slot(jax.random.fold_in(keys[13], 71), 0)
    return dict(right_side=right_side, block_weight=block_weight, across_weight=across_weight, along_weight=along_weight, block_stiffness=block_stiffness, across_matrix=across_matrix, along_matrix=along_matrix, boundary_blocks=boundary_blocks, block_rows=block_rows, block_columns=block_columns, live_pairs=live_pairs, surface_index=surface_index, interface_slot=interface_slot)


def product(left, right):
    return jnp.einsum('cabk,kl->cabl', left.astype(jnp.float32), right.astype(jnp.float32))


def stiffness_piece(rounded, block_weight, across_weight, along_weight, block_stiffness, across_matrix, along_matrix):
    padded = jnp.pad(rounded, ((0, 0), (1, 1), (1, 1), (0, 0)))
    across_padded = jnp.pad(across_weight, ((1, 1), (1, 1)))
    along_padded = jnp.pad(along_weight, ((1, 1), (1, 1)))
    result = block_weight[None, :, :, None] * product(rounded, block_stiffness)
    result = result - across_weight[None, :, :, None] * product(padded[:, 2:, 1:-1], across_matrix)
    result = result - across_padded[None, :-2, 1:-1, None] * product(padded[:, :-2, 1:-1], across_matrix.T)
    result = result - along_weight[None, :, :, None] * product(padded[:, 1:-1, 2:], along_matrix)
    result = result - along_padded[None, 1:-1, :-2, None] * product(padded[:, 1:-1, :-2], along_matrix.T)
    return result


def stiffness_apply(rounded, block_weight, across_weight, along_weight, block_stiffness, across_matrix, along_matrix):
    group = math.gcd(CASES, 8)
    pieces = rounded.reshape(CASES // group, group, NBX, NBY, P_SIZE)

    def single(piece):
        return stiffness_piece(piece, block_weight, across_weight, along_weight, block_stiffness, across_matrix, along_matrix)

    return lax.map(single, pieces).reshape(CASES, NBX, NBY, P_SIZE)


def to_devices(field):
    shaped = field.reshape(CASES, N_SEC * N_CLU, BX, N_BLK, BY, P_SIZE)
    return shaped.transpose(1, 3, 0, 2, 4, 5).reshape(N_SEC * N_CLU, N_BLK, CASES, BX * BY * P_SIZE)


def from_devices(stacked):
    shaped = stacked.reshape(N_SEC * N_CLU, N_BLK, CASES, BX, BY, P_SIZE)
    return shaped.transpose(2, 0, 3, 1, 4, 5).reshape(CASES, NBX, NBY, P_SIZE)


def boundary_apply(rounded, boundary_blocks, block_rows, block_columns, live_pairs, surface_index, interface_slot):
    stacked = to_devices(rounded)
    surface = surface_index.reshape(N_SEC * N_CLU, N_BLK, SURF)
    traces = jax.vmap(jax.vmap(lambda field, picks: jnp.take(field, picks, axis=1)))(stacked, surface)
    traces = traces.reshape(N_SEC, N_CLU, N_BLK, CASES, SURF).transpose(1, 3, 0, 2, 4).reshape(N_CLU, CASES, RROWS)
    slots = interface_slot.reshape(N_CLU, RROWS)
    interface = jax.vmap(lambda trace, picks: jnp.take(trace, picks, axis=1))(traces, slots)
    row_tiles = interface.reshape(N_CLU, CASES, RCL, CL)
    device_count = N_SEC * N_CLU * N_BLK
    blocks = boundary_blocks.reshape(device_count, NP, CL, CL)
    rows_list = block_rows.reshape(device_count, NP)
    columns_list = block_columns.reshape(device_count, NP)
    live_list = live_pairs.reshape(device_count)
    indices = jnp.arange(device_count, dtype=jnp.int32)
    clu_of = (indices // N_BLK) % N_CLU
    blk_of = indices % N_BLK
    pair_index = jnp.arange(NP, dtype=jnp.int32)

    def column_step(total, item):
        block, rows, columns, live, clu, blk = item
        picked = jnp.take(row_tiles[clu], rows, axis=1)
        terms = jnp.einsum('cpk,pkl->cpl', picked.astype(jnp.float32), block.astype(jnp.float32))
        terms = terms * (pair_index < live).astype(jnp.float32)[None, :, None]
        return total.at[:, blk * CCL + columns].add(terms), None

    start_columns = jnp.zeros((CASES, N_BLK * CCL, CL), jnp.float32)
    column_total, _ = lax.scan(column_step, start_columns, (blocks, rows_list, columns_list, live_list, clu_of, blk_of))
    column_low = column_total.astype(jnp.bfloat16)

    def row_step(total, item):
        block, rows, columns, live, clu, blk = item
        picked = jnp.take(column_low, blk * CCL + columns, axis=1)
        terms = jnp.einsum('cpl,pkl->cpk', picked.astype(jnp.float32), block.astype(jnp.float32))
        terms = terms * (pair_index < live).astype(jnp.float32)[None, :, None]
        return total.at[:, clu * RCL + rows].add(terms), None

    start_rows = jnp.zeros((CASES, N_CLU * RCL, CL), jnp.float32)
    row_total, _ = lax.scan(row_step, start_rows, (blocks, rows_list, columns_list, live_list, clu_of, blk_of))
    ranges = row_total.reshape(CASES, N_CLU, RROWS).transpose(1, 0, 2)
    inverse = jax.vmap(lambda picks: jnp.zeros((RROWS,), jnp.int32).at[picks].set(jnp.arange(RROWS, dtype=jnp.int32)))(slots)
    slot_values = jax.vmap(lambda values, picks: jnp.take(values, picks, axis=1))(ranges, inverse)
    slot_values = slot_values.reshape(N_CLU, CASES, N_SEC, N_BLK, SURF).transpose(2, 0, 3, 1, 4)
    slot_values = slot_values.reshape(N_SEC * N_CLU, N_BLK, CASES, SURF)
    empty = jnp.zeros((N_SEC * N_CLU, N_BLK, CASES, BX * BY * P_SIZE), jnp.float32)
    filled = jax.vmap(jax.vmap(lambda field, picks, values: field.at[:, picks].add(values)))(empty, surface, slot_values)
    return from_devices(filled)


def reference(right_side, block_weight, across_weight, along_weight, block_stiffness, across_matrix, along_matrix, boundary_blocks, block_rows, block_columns, live_pairs, surface_index, interface_slot):
    solution = jnp.zeros_like(right_side)
    residual = right_side
    direction = right_side
    norm_now = jnp.sum(residual * residual, axis=(1, 2, 3))
    for iteration in range(ITERS):
        rounded = direction.astype(jnp.bfloat16)
        image_field = stiffness_apply(rounded, block_weight, across_weight, along_weight, block_stiffness, across_matrix, along_matrix)
        image_field = image_field + boundary_apply(rounded, boundary_blocks, block_rows, block_columns, live_pairs, surface_index, interface_slot)
        curvature = jnp.sum(direction * image_field, axis=(1, 2, 3))
        alpha = (norm_now / curvature)[:, None, None, None]
        solution = solution + alpha * direction
        residual = residual - alpha * image_field
        norm_next = jnp.sum(residual * residual, axis=(1, 2, 3))
        direction = residual + (norm_next / norm_now)[:, None, None, None] * direction
        norm_now = norm_next
    return solution
```

```python
import functools

import jax
import jax.numpy as jnp
from jax import lax
from jax.experimental import pallas as pl
from jax.experimental.pallas import tpu as pltpu
from jax.sharding import PartitionSpec as P

ITERS = 3
F32 = jnp.float32
BF16 = jnp.bfloat16
MESH = pl.DeviceIdType.MESH

TRACE, ZSUM, ZALL, YSUM, DOTS, UP, DOWN, LEFT, RIGHT = range(9)


def lanes(tile, index):
    return jnp.take_along_axis(tile, index, axis=1, mode="promise_in_bounds")


def kernel(
    axes,
    dims,
    rhs,
    weight,
    across,
    along,
    stiff,
    amat,
    lmat,
    blocks,
    rows,
    cols,
    live,
    surf,
    surf_inv,
    slot,
    slot_inv,
    out,
    direction,
    residual,
    image,
    total,
    rounded,
    side,
    across_ext,
    along_ext,
    traces,
    tiles,
    zpart,
    zrecv,
    zlow,
    ytile,
    ypart,
    yrecv,
    dot_send,
    dot_recv,
    send_sem,
    recv_sem,
    edge_send,
    edge_recv,
):
    n_sec, n_clu, n_blk = axes
    cases, bx, by, wide, pairs = dims
    n_slab, n_grp, n_all = n_sec * n_clu, n_sec * n_blk, n_sec * n_clu * n_blk
    sec, clu, blk = lax.axis_index("sec"), lax.axis_index("clu"), lax.axis_index("blk")
    slab = sec * n_clu + clu
    group = sec * n_blk + blk
    me = slab * n_blk + blk
    tile = (cases, wide)

    def slab_device(index):
        return (index // n_clu, lax.rem(index, n_clu), blk)

    def group_device(index):
        return (index // n_blk, clu, lax.rem(index, n_blk))

    def any_device(index):
        return (index // (n_clu * n_blk), lax.rem(index // n_blk, n_clu), lax.rem(index, n_blk))

    next_slab = slab_device(lax.rem(slab + 1, n_slab))
    last_slab = slab_device(lax.rem(slab + n_slab - 1, n_slab))
    next_blk = (sec, clu, lax.rem(blk + 1, n_blk))
    last_blk = (sec, clu, lax.rem(blk + n_blk - 1, n_blk))

    barrier = pltpu.get_barrier_semaphore()

    @pl.loop(1, n_all)
    def _(k):
        pl.semaphore_signal(
            barrier, inc=1, device_id=any_device(lax.rem(me + k, n_all)), device_id_type=MESH
        )

    def send(src, dst, it, phase, device):
        pltpu.make_async_remote_copy(
            src_ref=src,
            dst_ref=dst,
            send_sem=send_sem.at[it, phase],
            recv_sem=recv_sem.at[it, phase],
            device_id=device,
            device_id_type=MESH,
        ).start()

    def received(ref, it, phase):
        pltpu.make_async_copy(ref, ref, recv_sem.at[it, phase]).wait()

    def sent(ref, it, phase):
        pltpu.make_async_copy(ref, ref, send_sem.at[it, phase]).wait()

    surf_row = jnp.broadcast_to(surf[...], tile)
    surf_lane = lax.rem(surf_row, wide)
    surf_block = surf_row // wide
    zero = jnp.zeros(tile, F32)

    def begin(a, carry):
        square, trace = carry
        for b in range(by):
            i = a * by + b
            value = rhs[pl.ds(i, cases, stride=bx * by), :]
            direction[a, b] = value
            residual[a, b] = value
            total[a, b] = zero
            rounded[0, a + 1, b] = value.astype(BF16)
            square += value * value
            trace = jnp.where(surf_block == i, lanes(value, surf_lane), trace)
        return square, trace

    square, trace = lax.fori_loop(0, bx, begin, (zero, zero))
    traces[0, 0] = trace.astype(BF16)
    across_ext[1:bx] = across[: bx - 1]
    across_ext[bx] = across[bx - 1] * (slab < n_slab - 1).astype(F32)
    along_ext[1:by] = along[: by - 1]
    along_ext[by] = along[by - 1] * (blk < n_blk - 1).astype(F32)

    pl.semaphore_wait(barrier, n_all - 1)

    edges = (
        (across.at[bx - 1], across_ext.at[0], 0, next_slab),
        (along.at[by - 1], along_ext.at[0], 1, next_blk),
    )

    def edge_copy(src, dst, n, device):
        return pltpu.make_async_remote_copy(
            src_ref=src,
            dst_ref=dst,
            send_sem=edge_send.at[n],
            recv_sem=edge_recv.at[n],
            device_id=device,
            device_id_type=MESH,
        )

    def permuted(index_row, count, source):
        lane = lax.rem(index_row, wide)
        part = index_row // wide

        def step(k, value):
            found, number = source(k)
            return jnp.where(part == number, lanes(found, lane), value)

        return lax.fori_loop(0, count, step, zero, unroll=count if count <= 8 else 1)

    def pair_sums(pick, into, count, flip):
        unit = 8 if pairs % 8 == 0 else 1

        def step(i, sums):
            sums = list(sums)
            for u in range(unit):
                e = i * unit + u
                left = pick(e)
                dims_ = (((1,), (1 if flip else 0,)), ((), ()))
                term = lax.dot_general(left, blocks[e], dims_, preferred_element_type=F32)
                goal = jnp.where(e < live[0, 0], into[0, e], -1)
                sums = [s + jnp.where(goal == q, term, zero) for q, s in enumerate(sums)]
            return tuple(sums)

        return lax.fori_loop(0, pairs // unit, step, (zero,) * count)

    sublane = lax.broadcasted_iota(jnp.int32, tile, 0)
    lane_id = lax.broadcasted_iota(jnp.int32, tile, 1)

    def iteration(it, square, first, last):
        @pl.loop(1, n_grp)
        def _(k):
            target = lax.rem(group + k, n_grp)
            send(traces.at[it, 0], traces.at[it, k], it, TRACE, group_device(target))

        send(rounded.at[it, bx], rounded.at[it, 0], it, UP, next_slab)
        send(rounded.at[it, 1], rounded.at[it, bx + 1], it, DOWN, last_slab)
        send(rounded.at[it, pl.ds(1, bx), by - 1], side.at[it, 0], it, RIGHT, next_blk)
        send(rounded.at[it, pl.ds(1, bx), 0], side.at[it, 1], it, LEFT, last_blk)

        @pl.loop(0, bx)
        def _(a):
            own = rounded[it, a + 1].reshape(by * cases, wide)
            part = jnp.dot(own, stiff[...], preferred_element_type=F32)
            image[a] = weight[a] * part.reshape(by, cases, wide)

        received(traces.at[it, pl.ds(1, n_grp - 1)], it, TRACE)

        @pl.loop(0, n_grp)
        def _(r):
            def source(k):
                return traces[it, k].astype(F32), lax.rem(group - k + n_grp, n_grp)

            index = jnp.broadcast_to(slot[pl.ds(r, 1), :], tile)
            tiles[r] = permuted(index, n_grp, source).astype(BF16)

        sums = pair_sums(lambda e: tiles[rows[0, e]], cols, n_slab, False)
        for q in range(n_slab):
            zpart[it, q] = sums[q]

        @pl.loop(1, n_slab)
        def _(k):
            target = lax.rem(slab + k, n_slab)
            send(zpart.at[it, target], zrecv.at[it, k - 1], it, ZSUM, slab_device(target))

        received(rounded.at[it, 0], it, UP)
        received(rounded.at[it, bx + 1], it, DOWN)
        received(side.at[it, 0], it, RIGHT)
        received(side.at[it, 1], it, LEFT)

        @pl.loop(0, bx)
        def _(a):
            after = rounded[it, a + 2].reshape(by * cases, wide)
            before = rounded[it, a].reshape(by * cases, wide)
            part = jnp.dot(after, amat[...], preferred_element_type=F32)
            value = image[a] - across_ext[a + 1] * part.reshape(by, cases, wide)
            part = lax.dot_general(
                before, amat[...], (((1,), (1,)), ((), ())), preferred_element_type=F32
            )
            image[a] = value - across_ext[a] * part.reshape(by, cases, wide)

        received(zrecv.at[it], it, ZSUM)
        column = zpart[it, slab]
        for k in range(n_slab - 1):
            column += zrecv[it, k]
        zlow[it, 0] = column.astype(BF16)

        @pl.loop(1, n_slab)
        def _(k):
            target = lax.rem(slab + k, n_slab)
            send(zlow.at[it, 0], zlow.at[it, k], it, ZALL, slab_device(target))

        @pl.loop(0, bx)
        def _(a):
            right = rounded[it, a + 1, pl.ds(1, by - 1)].reshape((by - 1) * cases, wide)
            left = rounded[it, a + 1, pl.ds(0, by - 1)].reshape((by - 1) * cases, wide)
            after = jnp.concatenate([right, side[it, 1, a]], axis=0)
            before = jnp.concatenate([side[it, 0, a], left], axis=0)
            part = jnp.dot(after, lmat[...], preferred_element_type=F32)
            value = image[a] - along_ext[pl.ds(1, by), a] * part.reshape(by, cases, wide)
            part = lax.dot_general(
                before, lmat[...], (((1,), (1,)), ((), ())), preferred_element_type=F32
            )
            image[a] = value - along_ext[pl.ds(0, by), a] * part.reshape(by, cases, wide)

        received(zlow.at[it, pl.ds(1, n_slab - 1)], it, ZALL)
        sums = pair_sums(
            lambda e: zlow[it, lax.rem(slab - cols[0, e] + n_slab, n_slab)], rows, n_grp, True
        )
        for r in range(n_grp):
            ytile[r] = sums[r]

        @pl.loop(0, n_grp)
        def _(g):
            index = jnp.broadcast_to(slot_inv[pl.ds(g, 1), :], tile)
            ypart[it, g] = permuted(index, n_grp, lambda k: (ytile[k], k))

        @pl.loop(1, n_grp)
        def _(k):
            target = lax.rem(group + k, n_grp)
            send(ypart.at[it, target], yrecv.at[it, k - 1], it, YSUM, group_device(target))

        received(yrecv.at[it], it, YSUM)
        own_y = ypart[it, group]
        for k in range(n_grp - 1):
            own_y += yrecv[it, k]

        def finish(a, carry):
            d_q, r_q, q_q = carry
            for b in range(by):
                index = jnp.broadcast_to(surf_inv[pl.ds(a * by + b, 1), :], tile)
                extra = lanes(own_y, jnp.maximum(index, 0))
                value = image[a, b] + jnp.where(index >= 0, extra, zero)
                image[a, b] = value
                d_q += direction[a, b] * value
                r_q += residual[a, b] * value
                q_q += value * value
            return d_q, r_q, q_q

        d_q, r_q, q_q = lax.fori_loop(0, bx, finish, (zero, zero, zero))

        packed = zero
        for m, value in enumerate((square, d_q, r_q, q_q)):
            case = jnp.broadcast_to(jnp.sum(value, axis=1, keepdims=True), tile)
            packed = jnp.where(lane_id == sublane + m * cases, case, packed)
        dot_send[it] = jnp.sum(packed, axis=0, keepdims=True)

        @pl.loop(1, n_all)
        def _(k):
            target = any_device(lax.rem(me + k, n_all))
            send(dot_send.at[it], dot_recv.at[it, k - 1], it, DOTS, target)

        received(dot_recv.at[it], it, DOTS)
        summed = dot_send[it] + jnp.sum(dot_recv[it], axis=0)
        summed = jnp.broadcast_to(summed, tile)

        def case_value(m):
            mine = jnp.where(lane_id == sublane + m * cases, summed, zero)
            return jnp.broadcast_to(jnp.sum(mine, axis=1, keepdims=True), tile)

        norm, d_q = case_value(0), case_value(1)
        alpha = norm / d_q
        if last:

            @pl.loop(0, bx)
            def _(a):
                for b in range(by):
                    value = total[a, b] + alpha * direction[a, b]
                    out[pl.ds(a * by + b, cases, stride=bx * by), :] = value

            return zero

        r_q, q_q = case_value(2), case_value(3)
        norm_next = norm - 2.0 * alpha * r_q + alpha * alpha * q_q
        beta = norm_next / norm

        def update(a, carry):
            square, trace = carry
            for b in range(by):
                old = direction[a, b]
                total[a, b] += alpha * old
                rest = residual[a, b] - alpha * image[a, b]
                residual[a, b] = rest
                square += rest * rest
                value = rest + beta * old
                direction[a, b] = value
                rounded[it + 1, a + 1, b] = value.astype(BF16)
                trace = jnp.where(surf_block == a * by + b, lanes(value, surf_lane), trace)
            return square, trace

        square, trace = lax.fori_loop(0, bx, update, (zero, zero))
        traces[it + 1, 0] = trace.astype(BF16)
        return square

    for edge in edges:
        edge_copy(*edge).start()
    for edge in edges:
        edge_copy(*edge).wait()
    across_ext[0] = across_ext[0] * (slab > 0).astype(F32)
    along_ext[0] = along_ext[0] * (blk > 0).astype(F32)

    square = lax.fori_loop(0, ITERS - 1, lambda it, s: iteration(it, s, False, False), square)
    iteration(ITERS - 1, square, False, True)

    @pl.loop(0, ITERS)
    def _(it):
        sent(traces.at[it, pl.ds(1, n_grp - 1)], it, TRACE)
        sent(rounded.at[it, 0], it, UP)
        sent(rounded.at[it, bx + 1], it, DOWN)
        sent(side.at[it, 0], it, RIGHT)
        sent(side.at[it, 1], it, LEFT)
        sent(zrecv.at[it], it, ZSUM)
        sent(zlow.at[it, pl.ds(1, n_slab - 1)], it, ZALL)
        sent(yrecv.at[it], it, YSUM)
        sent(dot_recv.at[it], it, DOTS)


def shards(axes, *args):
    (
        right_side,
        block_weight,
        across_weight,
        along_weight,
        block_stiffness,
        across_matrix,
        along_matrix,
        boundary_blocks,
        block_rows,
        block_columns,
        live_pairs,
        surface_index,
        interface_slot,
    ) = args
    cases, bx, by, wide = right_side.shape
    pairs = block_rows.shape[-1]
    slots = interface_slot.shape[0]
    surface = surface_index.reshape(-1)
    n_sec, n_clu, n_blk = axes
    n_slab, n_grp, n_all = n_sec * n_clu, n_sec * n_blk, n_sec * n_clu * n_blk
    number = jnp.arange(slots, dtype=jnp.int32)
    slot_inv = jnp.sum(
        jnp.where(interface_slot[:, None] == number[None, :], number[:, None], 0), axis=0
    )
    dofs = jnp.arange(bx * by * wide, dtype=jnp.int32)
    order = jnp.arange(1, wide + 1, dtype=jnp.int32)
    surf_inv = (
        jnp.sum(jnp.where(surface[:, None] == dofs[None, :], order[:, None], 0), axis=0) - 1
    )

    def spread(factor):
        return jnp.broadcast_to(factor[:, :, None, None], factor.shape + (1, wide))

    vmem = pl.BlockSpec(memory_space=pltpu.VMEM)
    smem = pl.BlockSpec(memory_space=pltpu.SMEM)
    field = pltpu.VMEM((bx, by, cases, wide), F32)
    result = pl.pallas_call(
        functools.partial(kernel, axes, (cases, bx, by, wide, pairs)),
        out_shape=jax.ShapeDtypeStruct((cases * bx * by, wide), F32),
        in_specs=[vmem] * 8 + [smem] * 3 + [vmem] * 4,
        out_specs=vmem,
        scratch_shapes=[
            field,
            field,
            field,
            field,
            pltpu.VMEM((ITERS, bx + 2, by, cases, wide), BF16),
            pltpu.VMEM((ITERS, 2, bx, cases, wide), BF16),
            pltpu.VMEM((bx + 1, by, 1, wide), F32),
            pltpu.VMEM((by + 1, bx, 1, wide), F32),
            pltpu.VMEM((ITERS, n_grp, cases, wide), BF16),
            pltpu.VMEM((n_grp, cases, wide), BF16),
            pltpu.VMEM((ITERS, n_slab, cases, wide), F32),
            pltpu.VMEM((ITERS, n_slab - 1, cases, wide), F32),
            pltpu.VMEM((ITERS, n_slab, cases, wide), BF16),
            pltpu.VMEM((n_grp, cases, wide), F32),
            pltpu.VMEM((ITERS, n_grp, cases, wide), F32),
            pltpu.VMEM((ITERS, n_grp - 1, cases, wide), F32),
            pltpu.VMEM((ITERS, 1, wide), F32),
            pltpu.VMEM((ITERS, n_all - 1, 1, wide), F32),
            pltpu.SemaphoreType.DMA((ITERS, 9)),
            pltpu.SemaphoreType.DMA((ITERS, 9)),
            pltpu.SemaphoreType.DMA((2,)),
            pltpu.SemaphoreType.DMA((2,)),
        ],
        compiler_params=pltpu.CompilerParams(
            collective_id=0, has_side_effects=True, vmem_limit_bytes=44 * 1024 * 1024
        ),
        name="conjugate_gradients",
    )(
        right_side.reshape(cases * bx * by, wide),
        spread(block_weight),
        spread(across_weight),
        spread(along_weight.T),
        block_stiffness,
        across_matrix,
        along_matrix,
        boundary_blocks.reshape(pairs, wide, wide),
        block_rows.reshape(1, pairs),
        block_columns.reshape(1, pairs),
        live_pairs.reshape(1, 1),
        surface.reshape(1, wide),
        surf_inv.reshape(bx * by, wide),
        interface_slot.reshape(n_grp, wide),
        slot_inv.reshape(n_grp, wide),
    )
    return result.reshape(right_side.shape)


def solution(mesh):
    axes = tuple(mesh.shape[name] for name in ("sec", "clu", "blk"))
    field = P(None, ("sec", "clu"), "blk", None)
    factor = P(("sec", "clu"), "blk")
    listed = P("sec", "clu", "blk")
    return jax.shard_map(
        functools.partial(shards, axes),
        mesh=mesh,
        in_specs=(
            field,
            factor,
            factor,
            factor,
            P(),
            P(),
            P(),
            P("sec", "clu", "blk", None, None),
            listed,
            listed,
            listed,
            listed,
            P("clu"),
        ),
        out_specs=field,
        check_vma=False,
    )
```

```python
import functools

import jax
import jax.numpy as jnp
from jax import lax
from jax.experimental import pallas as pl
from jax.experimental.pallas import tpu as pltpu
from jax.sharding import PartitionSpec as P

ITERS = 3
F32 = jnp.float32
BF16 = jnp.bfloat16
MESH = pl.DeviceIdType.MESH

TRACE, ZSUM, ZALL, YSUM, DOTS, UP, DOWN, LEFT, RIGHT = range(9)


def lanes(tile, index):
    return jnp.take_along_axis(tile, index, axis=1, mode="promise_in_bounds")


def kernel(
    axes,
    dims,
    rhs_hbm,
    weight_hbm,
    across_hbm,
    along_hbm,
    stiff_hbm,
    amat_hbm,
    lmat_hbm,
    blocks_hbm,
    surf_hbm,
    slot_hbm,
    rows_hbm,
    cols_hbm,
    live_hbm,
    out,
    rhs,
    weight_in,
    across_in,
    along_in,
    stiff,
    amat,
    lmat,
    blocks,
    surf,
    slot,
    rows,
    cols,
    live,
    weight,
    surf_inv,
    slot_col,
    slot_inv,
    direction,
    residual,
    image,
    total,
    rounded,
    side,
    across_ext,
    along_ext,
    traces,
    tiles,
    zpart,
    zrecv,
    zlow,
    ytile,
    ypart,
    yrecv,
    dot_send,
    dot_recv,
    send_sem,
    recv_sem,
    edge_send,
    edge_recv,
    load_sem,
):
    n_sec, n_clu, n_blk = axes
    cases, bx, by, wide, pairs = dims
    n_slab, n_grp, n_all = n_sec * n_clu, n_sec * n_blk, n_sec * n_clu * n_blk
    sec, clu, blk = lax.axis_index("sec"), lax.axis_index("clu"), lax.axis_index("blk")
    slab = sec * n_clu + clu
    group = sec * n_blk + blk
    me = slab * n_blk + blk
    tile = (cases, wide)

    def turned(position, count, by_):
        value = position + by_
        return jnp.where(value >= count, value - count, value)

    secs = [sec if k == 0 else turned(sec, n_sec, k) for k in range(n_sec)]
    clus = [clu if k == 0 else turned(clu, n_clu, k) for k in range(n_clu)]
    blks = [blk if k == 0 else turned(blk, n_blk, k) for k in range(n_blk)]
    slab_peers = [
        (secs[s] * n_clu + clus[c], (secs[s], clus[c], blk))
        for s in range(n_sec)
        for c in range(n_clu)
        if s or c
    ]
    group_peers = [
        (secs[s] * n_blk + blks[j], (secs[s], clu, blks[j]))
        for s in range(n_sec)
        for j in range(n_blk)
        if s or j
    ]
    all_peers = [
        (secs[s], clus[c], blks[j])
        for s in range(n_sec)
        for c in range(n_clu)
        for j in range(n_blk)
        if s or c or j
    ]

    def slab_device(index):
        return (index // n_clu, lax.rem(index, n_clu), blk)

    next_slab = slab_device(lax.rem(slab + 1, n_slab))
    last_slab = slab_device(lax.rem(slab + n_slab - 1, n_slab))
    next_blk = (sec, clu, lax.rem(blk + 1, n_blk))
    last_blk = (sec, clu, lax.rem(blk + n_blk - 1, n_blk))

    loads = [
        pltpu.make_async_copy(src, dst, load_sem.at[n])
        for n, (src, dst) in enumerate(
            (
                (rhs_hbm, rhs),
                (surf_hbm, surf),
                (across_hbm, across_in),
                (along_hbm, along_in),
                (weight_hbm, weight_in),
                (slot_hbm, slot),
                (rows_hbm, rows),
                (cols_hbm, cols),
                (live_hbm, live),
                (stiff_hbm, stiff),
                (amat_hbm, amat),
                (lmat_hbm, lmat),
                (blocks_hbm, blocks),
            )
        )
    ]
    for load in loads:
        load.start()

    barrier = pltpu.get_barrier_semaphore()
    for device in all_peers:
        pl.semaphore_signal(barrier, inc=1, device_id=device, device_id_type=MESH)

    def send(src, dst, it, phase, device):
        pltpu.make_async_remote_copy(
            src_ref=src,
            dst_ref=dst,
            send_sem=send_sem.at[it, phase],
            recv_sem=recv_sem.at[it, phase],
            device_id=device,
            device_id_type=MESH,
        ).start()

    def received(ref, it, phase):
        pltpu.make_async_copy(ref, ref, recv_sem.at[it, phase]).wait()

    def sent(ref, it, phase):
        pltpu.make_async_copy(ref, ref, send_sem.at[it, phase]).wait()

    for load in loads[:5]:
        load.wait()
    surf_row = jnp.broadcast_to(surf[...], tile)
    surf_lane = lax.rem(surf_row, wide)
    surf_block = surf_row // wide
    zero = jnp.zeros(tile, F32)

    def begin(a, carry):
        square, trace = carry
        for b in range(by):
            i = a * by + b
            value = rhs[pl.ds(i, cases, stride=bx * by), :]
            direction[a, b] = value
            residual[a, b] = value
            total[a, b] = zero
            rounded[0, a + 1, b] = value.astype(BF16)
            square += value * value
            trace = jnp.where(surf_block == i, lanes(value, surf_lane), trace)
        return square, trace

    square, start = lax.fori_loop(0, bx, begin, (zero, zero), unroll=2)
    traces[0, group] = start.astype(BF16)
    inner_slab = (slab < n_slab - 1).astype(F32)
    inner_blk = (blk < n_blk - 1).astype(F32)
    for b in range(by):
        shape = (bx, wide)
        own_w = jnp.broadcast_to(weight_in[:, b : b + 1], shape)
        own_a = jnp.broadcast_to(across_in[:, b : b + 1], shape)
        own_l = jnp.broadcast_to(along_in[:, b : b + 1], shape)
        for a in range(bx):
            weight[a, b] = own_w[a : a + 1]
            across_ext[a + 1, b] = own_a[a : a + 1]
            along_ext[b + 1, a] = own_l[a : a + 1]

    pl.semaphore_wait(barrier, n_all - 1)

    edges = (
        (across_ext.at[bx], across_ext.at[0], 0, next_slab),
        (along_ext.at[by], along_ext.at[0], 1, next_blk),
    )

    def edge_copy(src, dst, n, device):
        return pltpu.make_async_remote_copy(
            src_ref=src,
            dst_ref=dst,
            send_sem=edge_send.at[n],
            recv_sem=edge_recv.at[n],
            device_id=device,
            device_id_type=MESH,
        )

    def permuted(index_row, count, source):
        lane = lax.rem(index_row, wide)
        part = index_row // wide

        def step(k, value):
            found, number = source(k)
            return jnp.where(part == number, lanes(found, lane), value)

        return lax.fori_loop(0, count, step, zero, unroll=count if count <= 8 else 1)

    def pair_sums(pick, into, count, flip):
        unit = 8 if pairs % 8 == 0 else 1

        def step(i, sums):
            sums = list(sums)
            for u in range(unit):
                e = i * unit + u
                left = pick(e)
                dims_ = (((1,), (1 if flip else 0,)), ((), ()))
                term = lax.dot_general(left, blocks[e], dims_, preferred_element_type=F32)
                goal = jnp.where(e < live[0, 0], into[0, e], -1)
                sums = [s + jnp.where(goal == q, term, zero) for q, s in enumerate(sums)]
            return tuple(sums)

        return lax.fori_loop(0, pairs // unit, step, (zero,) * count, unroll=2)

    sublane = lax.broadcasted_iota(jnp.int32, tile, 0)
    lane_id = lax.broadcasted_iota(jnp.int32, tile, 1)

    def begin_sends(it):
        for _, device in group_peers:
            send(traces.at[it, group], traces.at[it, group], it, TRACE, device)
        send(rounded.at[it, bx], rounded.at[it, 0], it, UP, next_slab)
        send(rounded.at[it, 1], rounded.at[it, bx + 1], it, DOWN, last_slab)
        send(rounded.at[it, pl.ds(1, bx), by - 1], side.at[it, 0], it, RIGHT, next_blk)
        send(rounded.at[it, pl.ds(1, bx), 0], side.at[it, 1], it, LEFT, last_blk)

    def iteration(it, square, d_surf, last):
        @pl.loop(0, bx, unroll=4)
        def _(a):
            own = rounded[it, a + 1].reshape(by * cases, wide)
            part = jnp.dot(own, stiff[...], preferred_element_type=F32)
            image[a] = weight[a] * part.reshape(by, cases, wide)

        received(traces.at[it, pl.ds(1, n_grp - 1)], it, TRACE)

        @pl.loop(0, n_grp, unroll=4)
        def _(r):
            def source(k):
                return traces[it, k].astype(F32), k

            index = jnp.broadcast_to(slot[pl.ds(r, 1), :], tile)
            tiles[r] = permuted(index, n_grp, source).astype(BF16)

        sums = pair_sums(lambda e: tiles[rows[0, e]], cols, n_slab, False)
        for q in range(n_slab):
            zpart[it, q] = sums[q]

        for k, (target, device) in enumerate(slab_peers):
            send(zpart.at[it, target], zrecv.at[it, k], it, ZSUM, device)

        @pl.when(it == 0)
        def _():
            for edge in edges:
                edge_copy(*edge).wait()
            across_ext[0] = across_ext[0] * (slab > 0).astype(F32)
            along_ext[0] = along_ext[0] * (blk > 0).astype(F32)
            across_ext[bx] = across_ext[bx] * inner_slab
            along_ext[by] = along_ext[by] * inner_blk

        received(rounded.at[it, 0], it, UP)
        received(rounded.at[it, bx + 1], it, DOWN)
        received(side.at[it, 0], it, RIGHT)
        received(side.at[it, 1], it, LEFT)

        @pl.loop(0, bx, unroll=4)
        def _(a):
            after = rounded[it, a + 2].reshape(by * cases, wide)
            before = rounded[it, a].reshape(by * cases, wide)
            part = jnp.dot(after, amat[...], preferred_element_type=F32)
            value = image[a] - across_ext[a + 1] * part.reshape(by, cases, wide)
            part = lax.dot_general(
                before, amat[...], (((1,), (1,)), ((), ())), preferred_element_type=F32
            )
            image[a] = value - across_ext[a] * part.reshape(by, cases, wide)

        received(zrecv.at[it], it, ZSUM)
        column = zpart[it, slab]
        for k in range(n_slab - 1):
            column += zrecv[it, k]
        zlow[it, slab] = column.astype(BF16)
        for _, device in slab_peers:
            send(zlow.at[it, slab], zlow.at[it, slab], it, ZALL, device)

        @pl.loop(0, bx, unroll=4)
        def _(a):
            right = rounded[it, a + 1, pl.ds(1, by - 1)].reshape((by - 1) * cases, wide)
            left = rounded[it, a + 1, pl.ds(0, by - 1)].reshape((by - 1) * cases, wide)
            after = jnp.concatenate([right, side[it, 1, a]], axis=0)
            before = jnp.concatenate([side[it, 0, a], left], axis=0)
            part = jnp.dot(after, lmat[...], preferred_element_type=F32)
            value = image[a] - along_ext[pl.ds(1, by), a] * part.reshape(by, cases, wide)
            part = lax.dot_general(
                before, lmat[...], (((1,), (1,)), ((), ())), preferred_element_type=F32
            )
            image[a] = value - along_ext[pl.ds(0, by), a] * part.reshape(by, cases, wide)

        received(zlow.at[it, pl.ds(1, n_slab - 1)], it, ZALL)
        sums = pair_sums(
            lambda e: zlow[it, cols[0, e]], rows, n_grp, True
        )
        for r in range(n_grp):
            ytile[r] = sums[r]

        @pl.loop(0, n_grp, unroll=4)
        def _(g):
            index = jnp.broadcast_to(slot_inv[pl.ds(g, 1), :], tile)
            ypart[it, g] = permuted(index, n_grp, lambda k: (ytile[k], k))

        for k, (target, device) in enumerate(group_peers):
            send(ypart.at[it, target], yrecv.at[it, k], it, YSUM, device)

        def finish(a, carry):
            d_q, r_q, q_q, r_surf, q_surf = carry
            for b in range(by):
                value = image[a, b]
                rest = residual[a, b]
                d_q += direction[a, b] * value
                r_q += rest * value
                q_q += value * value
                here = surf_block == a * by + b
                r_surf = jnp.where(here, lanes(rest, surf_lane), r_surf)
                q_surf = jnp.where(here, lanes(value, surf_lane), q_surf)
            return d_q, r_q, q_q, r_surf, q_surf

        d_q, r_q, q_q, r_surf, q_surf = lax.fori_loop(0, bx, finish, (zero,) * 5, unroll=2)

        received(yrecv.at[it], it, YSUM)
        own_y = ypart[it, group]
        for k in range(n_grp - 1):
            own_y += yrecv[it, k]
        d_q += d_surf * own_y
        r_q += r_surf * own_y
        q_q += (2.0 * q_surf + own_y) * own_y

        packed = zero
        for m, value in enumerate((square, d_q, r_q, q_q)):
            case = jnp.broadcast_to(jnp.sum(value, axis=1, keepdims=True), tile)
            packed = jnp.where(lane_id == sublane + m * cases, case, packed)
        dot_send[it] = jnp.sum(packed, axis=0, keepdims=True)

        for k, device in enumerate(all_peers):
            send(dot_send.at[it], dot_recv.at[it, k], it, DOTS, device)

        if not last:

            @pl.loop(0, bx, unroll=2)
            def _(a):
                for b in range(by):
                    index = jnp.broadcast_to(surf_inv[pl.ds(a * by + b, 1), :], tile)
                    extra = lanes(own_y, jnp.maximum(index, 0))
                    image[a, b] += jnp.where(index >= 0, extra, zero)

        received(dot_recv.at[it], it, DOTS)
        summed = dot_send[it] + jnp.sum(dot_recv[it], axis=0)
        summed = jnp.broadcast_to(summed, tile)

        def case_value(m):
            mine = jnp.where(lane_id == sublane + m * cases, summed, zero)
            return jnp.broadcast_to(jnp.sum(mine, axis=1, keepdims=True), tile)

        norm, d_q = case_value(0), case_value(1)
        alpha = norm / d_q
        if last:

            @pl.loop(0, bx, unroll=2)
            def _(a):
                for b in range(by):
                    value = total[a, b] + alpha * direction[a, b]
                    out[pl.ds(a * by + b, cases, stride=bx * by), :] = value

            return zero, zero

        r_q, q_q = case_value(2), case_value(3)
        norm_next = norm - 2.0 * alpha * r_q + alpha * alpha * q_q
        beta = norm_next / norm

        def update(a, carry):
            square, trace = carry
            for b in range(by):
                old = direction[a, b]
                total[a, b] += alpha * old
                rest = residual[a, b] - alpha * image[a, b]
                residual[a, b] = rest
                square += rest * rest
                value = rest + beta * old
                direction[a, b] = value
                rounded[it + 1, a + 1, b] = value.astype(BF16)
                trace = jnp.where(surf_block == a * by + b, lanes(value, surf_lane), trace)
            return square, trace

        square, trace = lax.fori_loop(0, bx, update, (zero, zero), unroll=2)
        traces[it + 1, group] = trace.astype(BF16)
        begin_sends(it + 1)
        return square, trace

    begin_sends(0)
    for edge in edges:
        edge_copy(*edge).start()
    for load in loads[5:]:
        load.wait()

    square_tile = (wide, wide)
    down = lax.broadcasted_iota(jnp.int32, square_tile, 0)
    over = lax.broadcasted_iota(jnp.int32, square_tile, 1)
    surf_col = jnp.broadcast_to(surf[...], square_tile).T

    @pl.loop(0, bx * by, unroll=4)
    def _(i):
        hit = jnp.where(surf_col == over + i * wide, down + 1, 0)
        surf_inv[pl.ds(i, 1), :] = jnp.sum(hit, axis=0, keepdims=True) - 1

    @pl.loop(0, n_grp)
    def _(r):
        slot_col[r] = jnp.broadcast_to(slot[pl.ds(r, 1), :], square_tile).T

    @pl.loop(0, n_grp)
    def _(g):
        def step(r, found):
            return jnp.where(slot_col[r] == over + g * wide, down + r * wide, found)

        found = lax.fori_loop(0, n_grp, step, jnp.zeros(square_tile, jnp.int32), unroll=4)
        slot_inv[pl.ds(g, 1), :] = jnp.sum(found, axis=0, keepdims=True)

    carry = lax.fori_loop(
        0, ITERS - 1, lambda it, c: iteration(it, c[0], c[1], False), (square, start)
    )
    iteration(ITERS - 1, carry[0], carry[1], True)

    @pl.loop(0, ITERS)
    def _(it):
        sent(traces.at[it, pl.ds(1, n_grp - 1)], it, TRACE)
        sent(rounded.at[it, 0], it, UP)
        sent(rounded.at[it, bx + 1], it, DOWN)
        sent(side.at[it, 0], it, RIGHT)
        sent(side.at[it, 1], it, LEFT)
        sent(zrecv.at[it], it, ZSUM)
        sent(zlow.at[it, pl.ds(1, n_slab - 1)], it, ZALL)
        sent(yrecv.at[it], it, YSUM)
        sent(dot_recv.at[it], it, DOTS)


def shards(axes, *args):
    (
        right_side,
        block_weight,
        across_weight,
        along_weight,
        block_stiffness,
        across_matrix,
        along_matrix,
        boundary_blocks,
        block_rows,
        block_columns,
        live_pairs,
        surface_index,
        interface_slot,
    ) = args
    cases, bx, by, wide = right_side.shape
    pairs = block_rows.shape[-1]
    surface = surface_index.reshape(-1)
    n_sec, n_clu, n_blk = axes
    n_slab, n_grp, n_all = n_sec * n_clu, n_sec * n_blk, n_sec * n_clu * n_blk
    hbm = pl.BlockSpec(memory_space=pltpu.HBM)
    vmem = pl.BlockSpec(memory_space=pltpu.VMEM)
    field = pltpu.VMEM((bx, by, cases, wide), F32)
    result = pl.pallas_call(
        functools.partial(kernel, axes, (cases, bx, by, wide, pairs)),
        out_shape=jax.ShapeDtypeStruct((cases * bx * by, wide), F32),
        in_specs=[hbm] * 13,
        out_specs=vmem,
        scratch_shapes=[
            pltpu.VMEM((cases * bx * by, wide), F32),
            pltpu.VMEM((bx, by), F32),
            pltpu.VMEM((bx, by), F32),
            pltpu.VMEM((bx, by), F32),
            pltpu.VMEM((wide, wide), BF16),
            pltpu.VMEM((wide, wide), BF16),
            pltpu.VMEM((wide, wide), BF16),
            pltpu.VMEM((pairs, wide, wide), BF16),
            pltpu.VMEM((1, wide), jnp.int32),
            pltpu.VMEM((n_grp, wide), jnp.int32),
            pltpu.SMEM((1, pairs), jnp.int32),
            pltpu.SMEM((1, pairs), jnp.int32),
            pltpu.SMEM((1, 1), jnp.int32),
            pltpu.VMEM((bx, by, 1, wide), F32),
            pltpu.VMEM((bx * by, wide), jnp.int32),
            pltpu.VMEM((n_grp, wide, wide), jnp.int32),
            pltpu.VMEM((n_grp, wide), jnp.int32),
            field,
            field,
            field,
            field,
            pltpu.VMEM((ITERS, bx + 2, by, cases, wide), BF16),
            pltpu.VMEM((ITERS, 2, bx, cases, wide), BF16),
            pltpu.VMEM((bx + 1, by, 1, wide), F32),
            pltpu.VMEM((by + 1, bx, 1, wide), F32),
            pltpu.VMEM((ITERS, n_grp, cases, wide), BF16),
            pltpu.VMEM((n_grp, cases, wide), BF16),
            pltpu.VMEM((ITERS, n_slab, cases, wide), F32),
            pltpu.VMEM((ITERS, n_slab - 1, cases, wide), F32),
            pltpu.VMEM((ITERS, n_slab, cases, wide), BF16),
            pltpu.VMEM((n_grp, cases, wide), F32),
            pltpu.VMEM((ITERS, n_grp, cases, wide), F32),
            pltpu.VMEM((ITERS, n_grp - 1, cases, wide), F32),
            pltpu.VMEM((ITERS, 1, wide), F32),
            pltpu.VMEM((ITERS, n_all - 1, 1, wide), F32),
            pltpu.SemaphoreType.DMA((ITERS, 9)),
            pltpu.SemaphoreType.DMA((ITERS, 9)),
            pltpu.SemaphoreType.DMA((2,)),
            pltpu.SemaphoreType.DMA((2,)),
            pltpu.SemaphoreType.DMA((13,)),
        ],
        compiler_params=pltpu.CompilerParams(
            collective_id=0, has_side_effects=True, vmem_limit_bytes=44 * 1024 * 1024
        ),
        name="conjugate_gradients",
    )(
        right_side.reshape(cases * bx * by, wide),
        block_weight,
        across_weight,
        along_weight,
        block_stiffness,
        across_matrix,
        along_matrix,
        boundary_blocks.reshape(pairs, wide, wide),
        surface.reshape(1, wide),
        interface_slot.reshape(n_grp, wide),
        block_rows.reshape(1, pairs),
        block_columns.reshape(1, pairs),
        live_pairs.reshape(1, 1),
    )
    return result.reshape(right_side.shape)


def solution(mesh):
    axes = tuple(mesh.shape[name] for name in ("sec", "clu", "blk"))
    field = P(None, ("sec", "clu"), "blk", None)
    factor = P(("sec", "clu"), "blk")
    listed = P("sec", "clu", "blk")
    return jax.shard_map(
        functools.partial(shards, axes),
        mesh=mesh,
        in_specs=(
            field,
            factor,
            factor,
            factor,
            P(),
            P(),
            P(),
            P("sec", "clu", "blk", None, None),
            listed,
            listed,
            listed,
            listed,
            P("clu"),
        ),
        out_specs=field,
        check_vma=False,
    )
```

```python
import functools

import jax
import jax.numpy as jnp
from jax import lax
from jax.experimental import pallas as pl
from jax.experimental.pallas import tpu as pltpu
from jax.sharding import PartitionSpec as P

ITERS = 3
F32 = jnp.float32
BF16 = jnp.bfloat16
MESH = pl.DeviceIdType.MESH

TRACE, ZSUM, ZALL, YSUM, DOTS, UP, DOWN, LEFT, RIGHT = range(9)


def lanes(tile, index):
    return jnp.take_along_axis(tile, index, axis=1, mode="promise_in_bounds")


def kernel(
    axes,
    dims,
    rhs_hbm,
    weight_hbm,
    across_hbm,
    along_hbm,
    stiff_hbm,
    amat_hbm,
    lmat_hbm,
    blocks_hbm,
    surf_hbm,
    slot_hbm,
    rows_hbm,
    cols_hbm,
    live_hbm,
    out,
    rhs,
    weight_in,
    across_in,
    along_in,
    stiff,
    amat,
    lmat,
    blocks,
    surf,
    slot,
    rows,
    cols,
    live,
    amat_t,
    lmat_t,
    blocks_t,
    weight,
    surf_inv,
    slot_col,
    slot_inv,
    direction,
    residual,
    image,
    total,
    rounded,
    side,
    across_ext,
    along_ext,
    traces,
    tiles,
    zpart,
    zrecv,
    zlow,
    ytile,
    ypart,
    yrecv,
    dot_send,
    dot_recv,
    send_sem,
    recv_sem,
    edge_send,
    edge_recv,
    load_sem,
):
    n_sec, n_clu, n_blk = axes
    cases, bx, by, wide, pairs = dims
    n_slab, n_grp, n_all = n_sec * n_clu, n_sec * n_blk, n_sec * n_clu * n_blk
    sec, clu, blk = lax.axis_index("sec"), lax.axis_index("clu"), lax.axis_index("blk")
    slab = sec * n_clu + clu
    group = sec * n_blk + blk
    me = slab * n_blk + blk
    tile = (cases, wide)

    def turned(position, count, by_):
        value = position + by_
        return jnp.where(value >= count, value - count, value)

    secs = [sec if k == 0 else turned(sec, n_sec, k) for k in range(n_sec)]
    clus = [clu if k == 0 else turned(clu, n_clu, k) for k in range(n_clu)]
    blks = [blk if k == 0 else turned(blk, n_blk, k) for k in range(n_blk)]
    slab_peers = [
        (secs[s] * n_clu + clus[c], (secs[s], clus[c], blk))
        for s in range(n_sec)
        for c in range(n_clu)
        if s or c
    ]
    group_peers = [
        (secs[s] * n_blk + blks[j], (secs[s], clu, blks[j]))
        for s in range(n_sec)
        for j in range(n_blk)
        if s or j
    ]
    all_peers = [
        (secs[s], clus[c], blks[j])
        for s in range(n_sec)
        for c in range(n_clu)
        for j in range(n_blk)
        if s or c or j
    ]

    def slab_device(index):
        return (index // n_clu, lax.rem(index, n_clu), blk)

    next_slab = slab_device(lax.rem(slab + 1, n_slab))
    last_slab = slab_device(lax.rem(slab + n_slab - 1, n_slab))
    next_blk = (sec, clu, lax.rem(blk + 1, n_blk))
    last_blk = (sec, clu, lax.rem(blk + n_blk - 1, n_blk))

    has_last, has_next = slab > 0, slab < n_slab - 1
    has_left, has_right = blk > 0, blk < n_blk - 1

    loads = [
        pltpu.make_async_copy(src, dst, load_sem.at[n])
        for n, (src, dst) in enumerate(
            (
                (rhs_hbm, rhs),
                (surf_hbm, surf),
                (across_hbm, across_in),
                (along_hbm, along_in),
                (weight_hbm, weight_in),
                (slot_hbm, slot),
                (rows_hbm, rows),
                (cols_hbm, cols),
                (live_hbm, live),
                (stiff_hbm, stiff),
                (amat_hbm, amat),
                (lmat_hbm, lmat),
                (blocks_hbm, blocks),
            )
        )
    ]
    for load in loads:
        load.start()

    barrier = pltpu.get_barrier_semaphore()
    for device in all_peers:
        pl.semaphore_signal(barrier, inc=1, device_id=device, device_id_type=MESH)

    def send(src, dst, it, phase, device):
        pltpu.make_async_remote_copy(
            src_ref=src,
            dst_ref=dst,
            send_sem=send_sem.at[it, phase],
            recv_sem=recv_sem.at[it, phase],
            device_id=device,
            device_id_type=MESH,
        ).start()

    def received(ref, it, phase):
        pltpu.make_async_copy(ref, ref, recv_sem.at[it, phase]).wait()

    def sent(ref, it, phase):
        pltpu.make_async_copy(ref, ref, send_sem.at[it, phase]).wait()

    for load in loads[:5]:
        load.wait()
    surf_row = jnp.broadcast_to(surf[...], tile)
    surf_lane = lax.rem(surf_row, wide)
    surf_block = surf_row // wide
    zero = jnp.zeros(tile, F32)

    def begin(a, carry):
        square, trace = carry
        for b in range(by):
            i = a * by + b
            value = rhs[pl.ds(i, cases, stride=bx * by), :]
            direction[a, b] = value
            residual[a, b] = value
            total[a, b] = zero
            rounded[0, a + 1, b] = value.astype(BF16)
            square += value * value
            trace = jnp.where(surf_block == i, lanes(value, surf_lane), trace)
        return square, trace

    square, start = lax.fori_loop(0, bx, begin, (zero, zero), unroll=2)
    traces[0, group] = start.astype(BF16)
    for there, ref in ((has_last, across_ext), (has_left, along_ext)):

        @pl.when(jnp.logical_not(there))
        def _(ref=ref):
            ref[0] = jnp.zeros(ref.shape[1:], F32)

    for it in range(ITERS):
        for there, halo, place in (
            (has_last, rounded, 0),
            (has_next, rounded, bx + 1),
            (has_left, side, 0),
            (has_right, side, 1),
        ):

            @pl.when(jnp.logical_not(there))
            def _(halo=halo, place=place, it=it):
                halo[it, place] = jnp.zeros(halo.shape[2:], BF16)

    for b in range(by):
        shape = (bx, wide)
        own_w = jnp.broadcast_to(weight_in[:, b : b + 1], shape)
        own_a = jnp.broadcast_to(across_in[:, b : b + 1], shape)
        own_l = jnp.broadcast_to(along_in[:, b : b + 1], shape)
        for a in range(bx):
            weight[a, b] = own_w[a : a + 1]
            across_ext[a + 1, b] = own_a[a : a + 1]
            along_ext[b + 1, a] = own_l[a : a + 1]

    pl.semaphore_wait(barrier, n_all - 1)

    edges = (
        (across_ext.at[bx], across_ext.at[0], 0, next_slab),
        (along_ext.at[by], along_ext.at[0], 1, next_blk),
    )

    def edge_copy(src, dst, n, device):
        return pltpu.make_async_remote_copy(
            src_ref=src,
            dst_ref=dst,
            send_sem=edge_send.at[n],
            recv_sem=edge_recv.at[n],
            device_id=device,
            device_id_type=MESH,
        )

    def permuted(index_row, count, source):
        lane = lax.rem(index_row, wide)
        part = index_row // wide

        def step(k, value):
            found, number = source(k)
            return jnp.where(part == number, lanes(found, lane), value)

        return lax.fori_loop(0, count, step, zero, unroll=count if count <= 8 else 1)

    def pair_sums(pick, into, count, flip):
        unit = 8 if pairs % 8 == 0 else 1

        def step(i, sums):
            sums = list(sums)
            for u in range(unit):
                e = i * unit + u
                left = pick(e)
                block = blocks_t[e] if flip else blocks[e]
                term = jnp.dot(left, block, preferred_element_type=F32)
                goal = jnp.where(e < live[0, 0, 0], into[0, e], -1)
                goal = jnp.full(tile, goal, jnp.int32)
                sums = [s + jnp.where(goal == q, term, zero) for q, s in enumerate(sums)]
            return tuple(sums)

        return lax.fori_loop(0, pairs // unit, step, (zero,) * count, unroll=2)

    sublane = lax.broadcasted_iota(jnp.int32, tile, 0)
    lane_id = lax.broadcasted_iota(jnp.int32, tile, 1)

    def begin_sends(it):
        for _, device in group_peers:
            send(traces.at[it, group], traces.at[it, group], it, TRACE, device)

        @pl.when(has_next)
        def _():
            send(rounded.at[it, bx], rounded.at[it, 0], it, UP, next_slab)

        @pl.when(has_last)
        def _():
            send(rounded.at[it, 1], rounded.at[it, bx + 1], it, DOWN, last_slab)

        @pl.when(has_right)
        def _():
            send(rounded.at[it, pl.ds(1, bx), by - 1], side.at[it, 0], it, RIGHT, next_blk)

        @pl.when(has_left)
        def _():
            send(rounded.at[it, pl.ds(1, bx), 0], side.at[it, 1], it, LEFT, last_blk)

    def iteration(it, square, d_surf, last):
        @pl.loop(0, bx, unroll=4)
        def _(a):
            own = rounded[it, a + 1].reshape(by * cases, wide)
            part = jnp.dot(own, stiff[...], preferred_element_type=F32)
            image[a] = weight[a] * part.reshape(by, cases, wide)

        received(traces.at[it, pl.ds(1, n_grp - 1)], it, TRACE)

        @pl.loop(0, n_grp, unroll=4)
        def _(r):
            def source(k):
                return traces[it, k].astype(F32), k

            index = jnp.broadcast_to(slot[pl.ds(r, 1), :], tile)
            tiles[r] = permuted(index, n_grp, source).astype(BF16)

        sums = pair_sums(lambda e: tiles[rows[0, e]], cols, n_slab, False)
        for q in range(n_slab):
            zpart[it, q] = sums[q]

        for k, (target, device) in enumerate(slab_peers):
            send(zpart.at[it, target], zrecv.at[it, k], it, ZSUM, device)

        @pl.when(it == 0)
        def _():
            for edge, onward, back in zip(edges, (has_next, has_right), (has_last, has_left)):

                @pl.when(onward)
                def _(edge=edge):
                    edge_copy(*edge).wait_send()

                @pl.when(back)
                def _(edge=edge):
                    edge_copy(*edge).wait_recv()

        for there, ref, phase in (
            (has_last, rounded.at[it, 0], UP),
            (has_next, rounded.at[it, bx + 1], DOWN),
            (has_left, side.at[it, 0], RIGHT),
            (has_right, side.at[it, 1], LEFT),
        ):

            @pl.when(there)
            def _(ref=ref, phase=phase):
                received(ref, it, phase)

        @pl.loop(0, bx, unroll=4)
        def _(a):
            after = rounded[it, a + 2].reshape(by * cases, wide)
            before = rounded[it, a].reshape(by * cases, wide)
            part = jnp.dot(after, amat[...], preferred_element_type=F32)
            value = image[a] - across_ext[a + 1] * part.reshape(by, cases, wide)
            part = jnp.dot(before, amat_t[...], preferred_element_type=F32)
            image[a] = value - across_ext[a] * part.reshape(by, cases, wide)

        received(zrecv.at[it], it, ZSUM)
        column = zpart[it, slab]
        for k in range(n_slab - 1):
            column += zrecv[it, k]
        zlow[it, slab] = column.astype(BF16)
        for _, device in slab_peers:
            send(zlow.at[it, slab], zlow.at[it, slab], it, ZALL, device)

        @pl.loop(0, bx, unroll=4)
        def _(a):
            right = rounded[it, a + 1, pl.ds(1, by - 1)].reshape((by - 1) * cases, wide)
            left = rounded[it, a + 1, pl.ds(0, by - 1)].reshape((by - 1) * cases, wide)
            after = jnp.concatenate([right, side[it, 1, a]], axis=0)
            before = jnp.concatenate([side[it, 0, a], left], axis=0)
            part = jnp.dot(after, lmat[...], preferred_element_type=F32)
            value = image[a] - along_ext[pl.ds(1, by), a] * part.reshape(by, cases, wide)
            part = jnp.dot(before, lmat_t[...], preferred_element_type=F32)
            image[a] = value - along_ext[pl.ds(0, by), a] * part.reshape(by, cases, wide)

        received(zlow.at[it, pl.ds(1, n_slab - 1)], it, ZALL)
        sums = pair_sums(
            lambda e: zlow[it, cols[0, e]], rows, n_grp, True
        )
        for r in range(n_grp):
            ytile[r] = sums[r]

        @pl.loop(0, n_grp, unroll=4)
        def _(g):
            index = jnp.broadcast_to(slot_inv[pl.ds(g, 1), :], tile)
            ypart[it, g] = permuted(index, n_grp, lambda k: (ytile[k], k))

        for k, (target, device) in enumerate(group_peers):
            send(ypart.at[it, target], yrecv.at[it, k], it, YSUM, device)

        def finish(a, carry):
            d_q, r_q, q_q, r_surf, q_surf = carry
            for b in range(by):
                value = image[a, b]
                rest = residual[a, b]
                d_q += direction[a, b] * value
                r_q += rest * value
                q_q += value * value
                here = surf_block == a * by + b
                r_surf = jnp.where(here, lanes(rest, surf_lane), r_surf)
                q_surf = jnp.where(here, lanes(value, surf_lane), q_surf)
            return d_q, r_q, q_q, r_surf, q_surf

        d_q, r_q, q_q, r_surf, q_surf = lax.fori_loop(0, bx, finish, (zero,) * 5, unroll=2)

        received(yrecv.at[it], it, YSUM)
        own_y = ypart[it, group]
        for k in range(n_grp - 1):
            own_y += yrecv[it, k]
        d_q += d_surf * own_y
        r_q += r_surf * own_y
        q_q += (2.0 * q_surf + own_y) * own_y

        packed = zero
        for m, value in enumerate((square, d_q, r_q, q_q)):
            case = jnp.broadcast_to(jnp.sum(value, axis=1, keepdims=True), tile)
            packed = jnp.where(lane_id == sublane + m * cases, case, packed)
        dot_send[it] = jnp.sum(packed, axis=0, keepdims=True)

        for k, device in enumerate(all_peers):
            send(dot_send.at[it], dot_recv.at[it, k], it, DOTS, device)

        if not last:

            @pl.loop(0, bx, unroll=2)
            def _(a):
                for b in range(by):
                    index = jnp.broadcast_to(surf_inv[pl.ds(a * by + b, 1), :], tile)
                    extra = lanes(own_y, jnp.maximum(index, 0))
                    image[a, b] += jnp.where(index >= 0, extra, zero)

        received(dot_recv.at[it], it, DOTS)
        summed = dot_send[it] + jnp.sum(dot_recv[it], axis=0)
        summed = jnp.broadcast_to(summed, tile)

        def case_value(m):
            mine = jnp.where(lane_id == sublane + m * cases, summed, zero)
            return jnp.broadcast_to(jnp.sum(mine, axis=1, keepdims=True), tile)

        norm, d_q = case_value(0), case_value(1)
        alpha = norm / d_q
        if last:

            @pl.loop(0, bx, unroll=2)
            def _(a):
                for b in range(by):
                    value = total[a, b] + alpha * direction[a, b]
                    out[pl.ds(a * by + b, cases, stride=bx * by), :] = value

            return zero, zero

        r_q, q_q = case_value(2), case_value(3)
        norm_next = norm - 2.0 * alpha * r_q + alpha * alpha * q_q
        beta = norm_next / norm

        def update(a, carry):
            square, trace = carry
            for b in range(by):
                old = direction[a, b]
                total[a, b] += alpha * old
                rest = residual[a, b] - alpha * image[a, b]
                residual[a, b] = rest
                square += rest * rest
                value = rest + beta * old
                direction[a, b] = value
                rounded[it + 1, a + 1, b] = value.astype(BF16)
                trace = jnp.where(surf_block == a * by + b, lanes(value, surf_lane), trace)
            return square, trace

        square, trace = lax.fori_loop(0, bx, update, (zero, zero), unroll=2)
        traces[it + 1, group] = trace.astype(BF16)
        begin_sends(it + 1)
        return square, trace

    begin_sends(0)
    for edge, onward in zip(edges, (has_next, has_right)):

        @pl.when(onward)
        def _(edge=edge):
            edge_copy(*edge).start()

    for load in loads[5:]:
        load.wait()

    amat_t[...] = amat[...].T
    lmat_t[...] = lmat[...].T

    @pl.loop(0, pairs, unroll=4)
    def _(e):
        blocks_t[e] = blocks[e].T

    square_tile = (wide, wide)
    down = lax.broadcasted_iota(jnp.int32, square_tile, 0)
    over = lax.broadcasted_iota(jnp.int32, square_tile, 1)
    surf_col = jnp.broadcast_to(surf[...], square_tile).T

    @pl.loop(0, bx * by, unroll=4)
    def _(i):
        hit = jnp.where(surf_col == over + i * wide, down + 1, 0)
        surf_inv[pl.ds(i, 1), :] = jnp.sum(hit, axis=0, keepdims=True) - 1

    @pl.loop(0, n_grp)
    def _(r):
        slot_col[r] = jnp.broadcast_to(slot[pl.ds(r, 1), :], square_tile).T

    @pl.loop(0, n_grp)
    def _(g):
        def step(r, found):
            return jnp.where(slot_col[r] == over + g * wide, down + r * wide, found)

        found = lax.fori_loop(0, n_grp, step, jnp.zeros(square_tile, jnp.int32), unroll=4)
        slot_inv[pl.ds(g, 1), :] = jnp.sum(found, axis=0, keepdims=True)

    carry = lax.fori_loop(
        0, ITERS - 1, lambda it, c: iteration(it, c[0], c[1], False), (square, start)
    )
    iteration(ITERS - 1, carry[0], carry[1], True)

    @pl.loop(0, ITERS)
    def _(it):
        sent(traces.at[it, pl.ds(1, n_grp - 1)], it, TRACE)
        for there, ref, phase in (
            (has_next, rounded.at[it, 0], UP),
            (has_last, rounded.at[it, bx + 1], DOWN),
            (has_right, side.at[it, 0], RIGHT),
            (has_left, side.at[it, 1], LEFT),
        ):

            @pl.when(there)
            def _(ref=ref, phase=phase):
                sent(ref, it, phase)
        sent(zrecv.at[it], it, ZSUM)
        sent(zlow.at[it, pl.ds(1, n_slab - 1)], it, ZALL)
        sent(yrecv.at[it], it, YSUM)
        sent(dot_recv.at[it], it, DOTS)


def shards(axes, *args):
    (
        right_side,
        block_weight,
        across_weight,
        along_weight,
        block_stiffness,
        across_matrix,
        along_matrix,
        boundary_blocks,
        block_rows,
        block_columns,
        live_pairs,
        surface_index,
        interface_slot,
    ) = args
    cases, bx, by, wide = right_side.shape
    pairs = block_rows.shape[-1]
    surface = surface_index.reshape(-1)
    n_sec, n_clu, n_blk = axes
    n_slab, n_grp, n_all = n_sec * n_clu, n_sec * n_blk, n_sec * n_clu * n_blk
    hbm = pl.BlockSpec(memory_space=pltpu.HBM)
    vmem = pl.BlockSpec(memory_space=pltpu.VMEM)
    field = pltpu.VMEM((bx, by, cases, wide), F32)
    result = pl.pallas_call(
        functools.partial(kernel, axes, (cases, bx, by, wide, pairs)),
        out_shape=jax.ShapeDtypeStruct((cases * bx * by, wide), F32),
        in_specs=[hbm] * 13,
        out_specs=vmem,
        scratch_shapes=[
            pltpu.VMEM((cases * bx * by, wide), F32),
            pltpu.VMEM((bx, by), F32),
            pltpu.VMEM((bx, by), F32),
            pltpu.VMEM((bx, by), F32),
            pltpu.VMEM((wide, wide), BF16),
            pltpu.VMEM((wide, wide), BF16),
            pltpu.VMEM((wide, wide), BF16),
            pltpu.VMEM((pairs, wide, wide), BF16),
            pltpu.VMEM((1, wide), jnp.int32),
            pltpu.VMEM((n_grp, wide), jnp.int32),
            pltpu.SMEM((1, pairs), jnp.int32),
            pltpu.SMEM((1, pairs), jnp.int32),
            pltpu.SMEM((1, 1, 1), jnp.int32),
            pltpu.VMEM((wide, wide), BF16),
            pltpu.VMEM((wide, wide), BF16),
            pltpu.VMEM((pairs, wide, wide), BF16),
            pltpu.VMEM((bx, by, 1, wide), F32),
            pltpu.VMEM((bx * by, wide), jnp.int32),
            pltpu.VMEM((n_grp, wide, wide), jnp.int32),
            pltpu.VMEM((n_grp, wide), jnp.int32),
            field,
            field,
            field,
            field,
            pltpu.VMEM((ITERS, bx + 2, by, cases, wide), BF16),
            pltpu.VMEM((ITERS, 2, bx, cases, wide), BF16),
            pltpu.VMEM((bx + 1, by, 1, wide), F32),
            pltpu.VMEM((by + 1, bx, 1, wide), F32),
            pltpu.VMEM((ITERS, n_grp, cases, wide), BF16),
            pltpu.VMEM((n_grp, cases, wide), BF16),
            pltpu.VMEM((ITERS, n_slab, cases, wide), F32),
            pltpu.VMEM((ITERS, n_slab - 1, cases, wide), F32),
            pltpu.VMEM((ITERS, n_slab, cases, wide), BF16),
            pltpu.VMEM((n_grp, cases, wide), F32),
            pltpu.VMEM((ITERS, n_grp, cases, wide), F32),
            pltpu.VMEM((ITERS, n_grp - 1, cases, wide), F32),
            pltpu.VMEM((ITERS, 1, wide), F32),
            pltpu.VMEM((ITERS, n_all - 1, 1, wide), F32),
            pltpu.SemaphoreType.DMA((ITERS, 9)),
            pltpu.SemaphoreType.DMA((ITERS, 9)),
            pltpu.SemaphoreType.DMA((2,)),
            pltpu.SemaphoreType.DMA((2,)),
            pltpu.SemaphoreType.DMA((13,)),
        ],
        compiler_params=pltpu.CompilerParams(
            collective_id=0, has_side_effects=True, vmem_limit_bytes=62 * 1024 * 1024
        ),
        name="conjugate_gradients",
    )(
        right_side.reshape(cases * bx * by, wide),
        block_weight,
        across_weight,
        along_weight,
        block_stiffness,
        across_matrix,
        along_matrix,
        boundary_blocks.reshape(pairs, wide, wide),
        surface.reshape(1, wide),
        interface_slot.reshape(n_grp, wide),
        block_rows.reshape(1, pairs),
        block_columns.reshape(1, pairs),
        live_pairs,
    )
    return result.reshape(right_side.shape)


def solution(mesh):
    axes = tuple(mesh.shape[name] for name in ("sec", "clu", "blk"))
    field = P(None, ("sec", "clu"), "blk", None)
    factor = P(("sec", "clu"), "blk")
    listed = P("sec", "clu", "blk")
    return jax.shard_map(
        functools.partial(shards, axes),
        mesh=mesh,
        in_specs=(
            field,
            factor,
            factor,
            factor,
            P(),
            P(),
            P(),
            P("sec", "clu", "blk", None, None),
            listed,
            listed,
            listed,
            listed,
            P("clu"),
        ),
        out_specs=field,
        check_vma=False,
    )
```

```python
import functools

import jax
import jax.numpy as jnp
from jax import lax
from jax.experimental import pallas as pl
from jax.experimental.pallas import tpu as pltpu
from jax.sharding import PartitionSpec as P

ITERS = 3
F32 = jnp.float32
BF16 = jnp.bfloat16
MESH = pl.DeviceIdType.MESH

TRACE, ZSUM, ZALL, YSUM, DOTS, UP, DOWN, LEFT, RIGHT = range(9)


def lanes(tile, index):
    return jnp.take_along_axis(tile, index, axis=1, mode="promise_in_bounds")


def kernel(
    axes,
    dims,
    rhs_hbm,
    weight_hbm,
    across_hbm,
    along_hbm,
    stiff_hbm,
    amat_hbm,
    lmat_hbm,
    blocks_hbm,
    surf_hbm,
    slot_hbm,
    rows_hbm,
    cols_hbm,
    live_hbm,
    out,
    rhs,
    weight_in,
    across_in,
    along_in,
    stiff,
    amat,
    lmat,
    blocks,
    surf,
    slot,
    rows,
    cols,
    live,
    amat_t,
    lmat_t,
    blocks_t,
    weight,
    surf_inv,
    slot_col,
    slot_inv,
    direction,
    residual,
    image,
    total,
    rounded,
    side,
    across_ext,
    along_ext,
    traces,
    tiles,
    zpart,
    zrecv,
    zlow,
    ytile,
    ypart,
    yrecv,
    dot_send,
    dot_recv,
    send_sem,
    recv_sem,
    edge_send,
    edge_recv,
    load_sem,
):
    n_sec, n_clu, n_blk = axes
    cases, bx, by, wide, pairs = dims
    n_slab, n_grp, n_all = n_sec * n_clu, n_sec * n_blk, n_sec * n_clu * n_blk
    sec, clu, blk = lax.axis_index("sec"), lax.axis_index("clu"), lax.axis_index("blk")
    slab = sec * n_clu + clu
    group = sec * n_blk + blk
    me = slab * n_blk + blk
    tile = (cases, wide)

    def turned(position, count, by_):
        value = position + by_
        return jnp.where(value >= count, value - count, value)

    secs = [sec if k == 0 else turned(sec, n_sec, k) for k in range(n_sec)]
    clus = [clu if k == 0 else turned(clu, n_clu, k) for k in range(n_clu)]
    blks = [blk if k == 0 else turned(blk, n_blk, k) for k in range(n_blk)]
    slab_peers = [
        (secs[s] * n_clu + clus[c], (secs[s], clus[c], blk))
        for s in range(n_sec)
        for c in range(n_clu)
        if s or c
    ]
    group_peers = [
        (secs[s] * n_blk + blks[j], (secs[s], clu, blks[j]))
        for s in range(n_sec)
        for j in range(n_blk)
        if s or j
    ]
    all_peers = [
        (secs[s], clus[c], blks[j])
        for s in range(n_sec)
        for c in range(n_clu)
        for j in range(n_blk)
        if s or c or j
    ]

    def slab_device(index):
        return (index // n_clu, lax.rem(index, n_clu), blk)

    next_slab = slab_device(lax.rem(slab + 1, n_slab))
    last_slab = slab_device(lax.rem(slab + n_slab - 1, n_slab))
    next_blk = (sec, clu, lax.rem(blk + 1, n_blk))
    last_blk = (sec, clu, lax.rem(blk + n_blk - 1, n_blk))

    has_last, has_next = slab > 0, slab < n_slab - 1
    has_left, has_right = blk > 0, blk < n_blk - 1

    loads = [
        pltpu.make_async_copy(src, dst, load_sem.at[n])
        for n, (src, dst) in enumerate(
            (
                (rhs_hbm, rhs),
                (surf_hbm, surf),
                (across_hbm, across_in),
                (along_hbm, along_in),
                (weight_hbm, weight_in),
                (slot_hbm, slot),
                (rows_hbm, rows),
                (cols_hbm, cols),
                (live_hbm, live),
                (stiff_hbm, stiff),
                (amat_hbm, amat),
                (lmat_hbm, lmat),
                (blocks_hbm, blocks),
            )
        )
    ]
    for load in loads:
        load.start()

    barrier = pltpu.get_barrier_semaphore()
    for device in all_peers:
        pl.semaphore_signal(barrier, inc=1, device_id=device, device_id_type=MESH)

    def send(src, dst, it, phase, device):
        pltpu.make_async_remote_copy(
            src_ref=src,
            dst_ref=dst,
            send_sem=send_sem.at[it, phase],
            recv_sem=recv_sem.at[it, phase],
            device_id=device,
            device_id_type=MESH,
        ).start()

    def received(ref, it, phase):
        pltpu.make_async_copy(ref, ref, recv_sem.at[it, phase]).wait()

    def sent(ref, it, phase):
        pltpu.make_async_copy(ref, ref, send_sem.at[it, phase]).wait()

    for load in loads[:5]:
        load.wait()
    surf_row = jnp.broadcast_to(surf[...], tile)
    surf_lane = lax.rem(surf_row, wide)
    surf_block = surf_row // wide
    zero = jnp.zeros(tile, F32)

    def begin(a, carry):
        square, trace = carry
        for b in range(by):
            i = a * by + b
            value = rhs[pl.ds(i, cases, stride=bx * by), :]
            direction[a, b] = value
            residual[a, b] = value
            total[a, b] = zero
            rounded[0, a + 1, b] = value.astype(BF16)
            square += value * value
            trace = jnp.where(surf_block == i, lanes(value, surf_lane), trace)
        return square, trace

    square, start = lax.fori_loop(0, bx, begin, (zero, zero), unroll=2)
    traces[0, group] = start.astype(BF16)
    for there, ref in ((has_last, across_ext), (has_left, along_ext)):

        @pl.when(jnp.logical_not(there))
        def _(ref=ref):
            ref[0] = jnp.zeros(ref.shape[1:], F32)

    for it in range(ITERS):
        for there, halo, place in (
            (has_last, rounded, 0),
            (has_next, rounded, bx + 1),
            (has_left, side, 0),
            (has_right, side, 1),
        ):

            @pl.when(jnp.logical_not(there))
            def _(halo=halo, place=place, it=it):
                halo[it, place] = jnp.zeros(halo.shape[2:], BF16)

    for b in range(by):
        shape = (bx, wide)
        own_w = jnp.broadcast_to(weight_in[:, b : b + 1], shape)
        own_a = jnp.broadcast_to(across_in[:, b : b + 1], shape)
        own_l = jnp.broadcast_to(along_in[:, b : b + 1], shape)
        for a in range(bx):
            weight[a, b] = own_w[a : a + 1]
            across_ext[a + 1, b] = own_a[a : a + 1]
            along_ext[b + 1, a] = own_l[a : a + 1]

    pl.semaphore_wait(barrier, n_all - 1)

    edges = (
        (across_ext.at[bx], across_ext.at[0], 0, next_slab),
        (along_ext.at[by], along_ext.at[0], 1, next_blk),
    )

    def edge_copy(src, dst, n, device):
        return pltpu.make_async_remote_copy(
            src_ref=src,
            dst_ref=dst,
            send_sem=edge_send.at[n],
            recv_sem=edge_recv.at[n],
            device_id=device,
            device_id_type=MESH,
        )

    def permuted(index_row, count, source):
        lane = index_row & (wide - 1)
        part = index_row // wide

        def step(k, value):
            found, number = source(k)
            return jnp.where(part == number, lanes(found, lane), value)

        return lax.fori_loop(0, count, step, zero, unroll=count if count <= 8 else 1)

    def pair_sums(pick, into, count, flip):
        unit = 8 if pairs % 8 == 0 else 1

        def step(i, sums):
            sums = list(sums)
            for u in range(unit):
                e = i * unit + u
                left = pick(e)
                block = blocks_t[e] if flip else blocks[e]
                term = jnp.dot(left, block, preferred_element_type=F32)
                goal = jnp.where(e < live[0, 0, 0], into[0, e], -1)
                goal = jnp.full(tile, goal, jnp.int32)
                sums = [s + jnp.where(goal == q, term, zero) for q, s in enumerate(sums)]
            return tuple(sums)

        return lax.fori_loop(0, pairs // unit, step, (zero,) * count, unroll=3)

    sublane = lax.broadcasted_iota(jnp.int32, tile, 0)
    lane_id = lax.broadcasted_iota(jnp.int32, tile, 1)

    def begin_sends(it):
        for _, device in group_peers:
            send(traces.at[it, group], traces.at[it, group], it, TRACE, device)

        @pl.when(has_next)
        def _():
            send(rounded.at[it, bx], rounded.at[it, 0], it, UP, next_slab)

        @pl.when(has_last)
        def _():
            send(rounded.at[it, 1], rounded.at[it, bx + 1], it, DOWN, last_slab)

        @pl.when(has_right)
        def _():
            send(rounded.at[it, pl.ds(1, bx), by - 1], side.at[it, 0], it, RIGHT, next_blk)

        @pl.when(has_left)
        def _():
            send(rounded.at[it, pl.ds(1, bx), 0], side.at[it, 1], it, LEFT, last_blk)

    def iteration(it, square, d_surf, last):
        @pl.loop(0, bx, unroll=4)
        def _(a):
            own = rounded[it, a + 1].reshape(by * cases, wide)
            part = jnp.dot(own, stiff[...], preferred_element_type=F32)
            image[a] = weight[a] * part.reshape(by, cases, wide)

        received(traces.at[it, pl.ds(1, n_grp - 1)], it, TRACE)

        @pl.loop(0, n_grp, unroll=4)
        def _(r):
            def source(k):
                return traces[it, k].astype(F32), k

            index = jnp.broadcast_to(slot[pl.ds(r, 1), :], tile)
            tiles[r] = permuted(index, n_grp, source).astype(BF16)

        sums = pair_sums(lambda e: tiles[rows[0, e]], cols, n_slab, False)
        for q in range(n_slab):
            zpart[it, q] = sums[q]

        for k, (target, device) in enumerate(slab_peers):
            send(zpart.at[it, target], zrecv.at[it, k], it, ZSUM, device)

        @pl.when(it == 0)
        def _():
            for edge, onward, back in zip(edges, (has_next, has_right), (has_last, has_left)):

                @pl.when(onward)
                def _(edge=edge):
                    edge_copy(*edge).wait_send()

                @pl.when(back)
                def _(edge=edge):
                    edge_copy(*edge).wait_recv()

        for there, ref, phase in (
            (has_last, rounded.at[it, 0], UP),
            (has_next, rounded.at[it, bx + 1], DOWN),
            (has_left, side.at[it, 0], RIGHT),
            (has_right, side.at[it, 1], LEFT),
        ):

            @pl.when(there)
            def _(ref=ref, phase=phase):
                received(ref, it, phase)

        @pl.loop(0, bx, unroll=4)
        def _(a):
            after = rounded[it, a + 2].reshape(by * cases, wide)
            before = rounded[it, a].reshape(by * cases, wide)
            part = jnp.dot(after, amat[...], preferred_element_type=F32)
            value = image[a] - across_ext[a + 1] * part.reshape(by, cases, wide)
            part = jnp.dot(before, amat_t[...], preferred_element_type=F32)
            image[a] = value - across_ext[a] * part.reshape(by, cases, wide)

        received(zrecv.at[it], it, ZSUM)
        column = zpart[it, slab]
        for k in range(n_slab - 1):
            column += zrecv[it, k]
        zlow[it, slab] = column.astype(BF16)
        for _, device in slab_peers:
            send(zlow.at[it, slab], zlow.at[it, slab], it, ZALL, device)

        @pl.loop(0, bx, unroll=4)
        def _(a):
            right = rounded[it, a + 1, pl.ds(1, by - 1)].reshape((by - 1) * cases, wide)
            left = rounded[it, a + 1, pl.ds(0, by - 1)].reshape((by - 1) * cases, wide)
            after = jnp.concatenate([right, side[it, 1, a]], axis=0)
            before = jnp.concatenate([side[it, 0, a], left], axis=0)
            part = jnp.dot(after, lmat[...], preferred_element_type=F32)
            value = image[a] - along_ext[pl.ds(1, by), a] * part.reshape(by, cases, wide)
            part = jnp.dot(before, lmat_t[...], preferred_element_type=F32)
            image[a] = value - along_ext[pl.ds(0, by), a] * part.reshape(by, cases, wide)

        received(zlow.at[it, pl.ds(1, n_slab - 1)], it, ZALL)
        sums = pair_sums(
            lambda e: zlow[it, cols[0, e]], rows, n_grp, True
        )
        for r in range(n_grp):
            ytile[r] = sums[r]

        @pl.loop(0, n_grp, unroll=4)
        def _(g):
            index = jnp.broadcast_to(slot_inv[pl.ds(g, 1), :], tile)
            ypart[it, g] = permuted(index, n_grp, lambda k: (ytile[k], k))

        for k, (target, device) in enumerate(group_peers):
            send(ypart.at[it, target], yrecv.at[it, k], it, YSUM, device)

        def finish(a, carry):
            d_q, r_q, q_q, r_surf, q_surf = carry
            for b in range(by):
                value = image[a, b]
                rest = residual[a, b]
                d_q += direction[a, b] * value
                if last:
                    continue
                r_q += rest * value
                q_q += value * value
                here = surf_block == a * by + b
                r_surf = jnp.where(here, lanes(rest, surf_lane), r_surf)
                q_surf = jnp.where(here, lanes(value, surf_lane), q_surf)
            return d_q, r_q, q_q, r_surf, q_surf

        d_q, r_q, q_q, r_surf, q_surf = lax.fori_loop(0, bx, finish, (zero,) * 5, unroll=2)

        received(yrecv.at[it], it, YSUM)
        own_y = ypart[it, group]
        for k in range(n_grp - 1):
            own_y += yrecv[it, k]
        d_q += d_surf * own_y
        r_q += r_surf * own_y
        q_q += (2.0 * q_surf + own_y) * own_y

        packed = zero
        for m, value in enumerate((square, d_q, r_q, q_q)):
            case = jnp.broadcast_to(jnp.sum(value, axis=1, keepdims=True), tile)
            packed = jnp.where(lane_id == sublane + m * cases, case, packed)
        dot_send[it] = jnp.sum(packed, axis=0, keepdims=True)

        for k, device in enumerate(all_peers):
            send(dot_send.at[it], dot_recv.at[it, k], it, DOTS, device)

        if not last:

            @pl.loop(0, bx, unroll=2)
            def _(a):
                for b in range(by):
                    index = jnp.broadcast_to(surf_inv[pl.ds(a * by + b, 1), :], tile)
                    extra = lanes(own_y, jnp.maximum(index, 0))
                    image[a, b] += jnp.where(index >= 0, extra, zero)

        received(dot_recv.at[it], it, DOTS)
        summed = dot_send[it] + jnp.sum(dot_recv[it], axis=0)
        summed = jnp.broadcast_to(summed, tile)

        def case_value(m):
            mine = jnp.where(lane_id == sublane + m * cases, summed, zero)
            return jnp.broadcast_to(jnp.sum(mine, axis=1, keepdims=True), tile)

        norm, d_q = case_value(0), case_value(1)
        alpha = norm / d_q
        if last:

            @pl.loop(0, bx, unroll=2)
            def _(a):
                for b in range(by):
                    value = total[a, b] + alpha * direction[a, b]
                    out[pl.ds(a * by + b, cases, stride=bx * by), :] = value

            return zero, zero

        r_q, q_q = case_value(2), case_value(3)
        norm_next = norm - 2.0 * alpha * r_q + alpha * alpha * q_q
        beta = norm_next / norm

        def update(a, carry):
            square, trace = carry
            for b in range(by):
                old = direction[a, b]
                total[a, b] += alpha * old
                rest = residual[a, b] - alpha * image[a, b]
                residual[a, b] = rest
                square += rest * rest
                value = rest + beta * old
                direction[a, b] = value
                rounded[it + 1, a + 1, b] = value.astype(BF16)
                trace = jnp.where(surf_block == a * by + b, lanes(value, surf_lane), trace)
            return square, trace

        square, trace = lax.fori_loop(0, bx, update, (zero, zero), unroll=2)
        traces[it + 1, group] = trace.astype(BF16)
        begin_sends(it + 1)
        return square, trace

    begin_sends(0)
    for edge, onward in zip(edges, (has_next, has_right)):

        @pl.when(onward)
        def _(edge=edge):
            edge_copy(*edge).start()

    for load in loads[5:]:
        load.wait()

    amat_t[...] = amat[...].T
    lmat_t[...] = lmat[...].T

    @pl.loop(0, pairs, unroll=4)
    def _(e):
        blocks_t[e] = blocks[e].T

    square_tile = (wide, wide)
    down = lax.broadcasted_iota(jnp.int32, square_tile, 0)
    over = lax.broadcasted_iota(jnp.int32, square_tile, 1)
    surf_col = jnp.broadcast_to(surf[...], square_tile).T

    @pl.loop(0, bx * by, unroll=4)
    def _(i):
        hit = jnp.where(surf_col == over + i * wide, down + 1, 0)
        surf_inv[pl.ds(i, 1), :] = jnp.sum(hit, axis=0, keepdims=True) - 1

    @pl.loop(0, n_grp)
    def _(r):
        slot_col[r] = jnp.broadcast_to(slot[pl.ds(r, 1), :], square_tile).T

    @pl.loop(0, n_grp)
    def _(g):
        def step(r, found):
            return jnp.where(slot_col[r] == over + g * wide, down + r * wide, found)

        found = lax.fori_loop(0, n_grp, step, jnp.zeros(square_tile, jnp.int32), unroll=4)
        slot_inv[pl.ds(g, 1), :] = jnp.sum(found, axis=0, keepdims=True)

    carry = lax.fori_loop(
        0, ITERS - 1, lambda it, c: iteration(it, c[0], c[1], False), (square, start)
    )
    iteration(ITERS - 1, carry[0], carry[1], True)

    @pl.loop(0, ITERS)
    def _(it):
        sent(traces.at[it, pl.ds(1, n_grp - 1)], it, TRACE)
        for there, ref, phase in (
            (has_next, rounded.at[it, 0], UP),
            (has_last, rounded.at[it, bx + 1], DOWN),
            (has_right, side.at[it, 0], RIGHT),
            (has_left, side.at[it, 1], LEFT),
        ):

            @pl.when(there)
            def _(ref=ref, phase=phase):
                sent(ref, it, phase)
        sent(zrecv.at[it], it, ZSUM)
        sent(zlow.at[it, pl.ds(1, n_slab - 1)], it, ZALL)
        sent(yrecv.at[it], it, YSUM)
        sent(dot_recv.at[it], it, DOTS)


def shards(axes, *args):
    (
        right_side,
        block_weight,
        across_weight,
        along_weight,
        block_stiffness,
        across_matrix,
        along_matrix,
        boundary_blocks,
        block_rows,
        block_columns,
        live_pairs,
        surface_index,
        interface_slot,
    ) = args
    cases, bx, by, wide = right_side.shape
    pairs = block_rows.shape[-1]
    surface = surface_index.reshape(-1)
    n_sec, n_clu, n_blk = axes
    n_slab, n_grp, n_all = n_sec * n_clu, n_sec * n_blk, n_sec * n_clu * n_blk
    hbm = pl.BlockSpec(memory_space=pltpu.HBM)
    vmem = pl.BlockSpec(memory_space=pltpu.VMEM)
    field = pltpu.VMEM((bx, by, cases, wide), F32)
    result = pl.pallas_call(
        functools.partial(kernel, axes, (cases, bx, by, wide, pairs)),
        out_shape=jax.ShapeDtypeStruct((cases * bx * by, wide), F32),
        in_specs=[hbm] * 13,
        out_specs=vmem,
        scratch_shapes=[
            pltpu.VMEM((cases * bx * by, wide), F32),
            pltpu.VMEM((bx, by), F32),
            pltpu.VMEM((bx, by), F32),
            pltpu.VMEM((bx, by), F32),
            pltpu.VMEM((wide, wide), BF16),
            pltpu.VMEM((wide, wide), BF16),
            pltpu.VMEM((wide, wide), BF16),
            pltpu.VMEM((pairs, wide, wide), BF16),
            pltpu.VMEM((1, wide), jnp.int32),
            pltpu.VMEM((n_grp, wide), jnp.int32),
            pltpu.SMEM((1, pairs), jnp.int32),
            pltpu.SMEM((1, pairs), jnp.int32),
            pltpu.SMEM((1, 1, 1), jnp.int32),
            pltpu.VMEM((wide, wide), BF16),
            pltpu.VMEM((wide, wide), BF16),
            pltpu.VMEM((pairs, wide, wide), BF16),
            pltpu.VMEM((bx, by, 1, wide), F32),
            pltpu.VMEM((bx * by, wide), jnp.int32),
            pltpu.VMEM((n_grp, wide, wide), jnp.int32),
            pltpu.VMEM((n_grp, wide), jnp.int32),
            field,
            field,
            field,
            field,
            pltpu.VMEM((ITERS, bx + 2, by, cases, wide), BF16),
            pltpu.VMEM((ITERS, 2, bx, cases, wide), BF16),
            pltpu.VMEM((bx + 1, by, 1, wide), F32),
            pltpu.VMEM((by + 1, bx, 1, wide), F32),
            pltpu.VMEM((ITERS, n_grp, cases, wide), BF16),
            pltpu.VMEM((n_grp, cases, wide), BF16),
            pltpu.VMEM((ITERS, n_slab, cases, wide), F32),
            pltpu.VMEM((ITERS, n_slab - 1, cases, wide), F32),
            pltpu.VMEM((ITERS, n_slab, cases, wide), BF16),
            pltpu.VMEM((n_grp, cases, wide), F32),
            pltpu.VMEM((ITERS, n_grp, cases, wide), F32),
            pltpu.VMEM((ITERS, n_grp - 1, cases, wide), F32),
            pltpu.VMEM((ITERS, 1, wide), F32),
            pltpu.VMEM((ITERS, n_all - 1, 1, wide), F32),
            pltpu.SemaphoreType.DMA((ITERS, 9)),
            pltpu.SemaphoreType.DMA((ITERS, 9)),
            pltpu.SemaphoreType.DMA((2,)),
            pltpu.SemaphoreType.DMA((2,)),
            pltpu.SemaphoreType.DMA((13,)),
        ],
        compiler_params=pltpu.CompilerParams(
            collective_id=0, has_side_effects=True, vmem_limit_bytes=62 * 1024 * 1024
        ),
        name="conjugate_gradients",
    )(
        right_side.reshape(cases * bx * by, wide),
        block_weight,
        across_weight,
        along_weight,
        block_stiffness,
        across_matrix,
        along_matrix,
        boundary_blocks.reshape(pairs, wide, wide),
        surface.reshape(1, wide),
        interface_slot.reshape(n_grp, wide),
        block_rows.reshape(1, pairs),
        block_columns.reshape(1, pairs),
        live_pairs,
    )
    return result.reshape(right_side.shape)


def solution(mesh):
    axes = tuple(mesh.shape[name] for name in ("sec", "clu", "blk"))
    field = P(None, ("sec", "clu"), "blk", None)
    factor = P(("sec", "clu"), "blk")
    listed = P("sec", "clu", "blk")
    return jax.shard_map(
        functools.partial(shards, axes),
        mesh=mesh,
        in_specs=(
            field,
            factor,
            factor,
            factor,
            P(),
            P(),
            P(),
            P("sec", "clu", "blk", None, None),
            listed,
            listed,
            listed,
            listed,
            P("clu"),
        ),
        out_specs=field,
        check_vma=False,
    )
```
